32 devices in a mesh: dp: 16 (over z, x, core), lon: 2 (over y).
Axes of the slice: x: 2, y: 2, z: 4, core: 2. Of those that a mesh axis runs over, the one named last changes fastest.
Arguments:
- features: bfloat16 [16, 18, 48, 1152], P('dp', 'lon'), may hold values from -6 to 6
- depth_w: bfloat16 [2, 3, 3, 1152], replicated, may hold values from -2 to 2
- point_w: bfloat16 [2, 1152, 256], replicated, may hold values from -0.1875 to 0.1875
- point_bias: float32 [2, 256], replicated, may hold values from -3 to 3
- cotangent: bfloat16 [16, 18, 48, 512], P('dp', 'lon'), may hold values from -6 to 6
Outputs:
- feature_grad: bfloat16 [16, 18, 48, 1152], P('dp', 'lon')
- depth_grad: bfloat16 [2, 3, 3, 1152], replicated
- point_grad: bfloat16 [2, 1152, 256], replicated
- bias_grad: float32 [2, 256], replicated
The draws below stay inside these ranges and needn't reach their ends.
All inputs are finite; a program needn't handle non-finite values.
Results may differ from the reference program's by a relative error of at most 0.0075.
Values may be sent and summed in bfloat16 or wider, within the bound.
A program may use at most 128 MiB of HBM per device.

```python
import jax
import jax.numpy as jnp
from jax import lax

LAT = 48
C = 1152
C_OUT = 256
RATE_A = 24
RATE_B = 36
IMGS = 16
LON = 18


def block_levels(stream_key, extent, pieces, low, top_value):
    loudness = 1.0
    for axis_at, parts in pieces:
        heights = jax.random.uniform(jax.random.fold_in(jax.random.fold_in(stream_key, 6), axis_at), (parts,), jnp.float32, low / len(pieces), top_value / len(pieces))
        loudness = loudness * jnp.repeat(jnp.exp(heights), extent[axis_at] // parts).reshape((-1,) + (1,) * (len(extent) - 1 - axis_at))
    return loudness


def gaussian(own_key, shape, scale, most, split=(), kind=jnp.bfloat16):
    gain = block_levels(own_key, shape, split, -0.22, 0.18) if split else 1.0
    drawn = jax.random.normal(own_key, shape, jnp.float32) * scale * gain
    return jnp.minimum(jnp.maximum(drawn, -most), most).astype(kind)


def setup_inputs(seed: int = 0) -> dict:
    arg_keys = jax.random.split(jax.random.key(seed), 6)
    features = gaussian(arg_keys[0], (IMGS, LON, LAT, C), 1.0, 6.0, ((0, 16), (1, 2)))
    depth_w = gaussian(arg_keys[1], (2, 3, 3, C), 9 ** -0.5, 2.0)
    point_w = gaussian(arg_keys[2], (2, C, C_OUT), C ** -0.5, 0.1875)
    point_bias = gaussian(arg_keys[3], (2, C_OUT), 0.5, 3.0, (), jnp.float32)
    cotangent = gaussian(arg_keys[4], (IMGS, LON, LAT, 2 * C_OUT), 1.0, 6.0, ((0, 16), (1, 2)))
    return {"features": features, "depth_w": depth_w, "point_w": point_w, "point_bias": point_bias, "cotangent": cotangent}


def lat_shift(grid_field, offset, axis_pos):
    height = grid_field.shape[axis_pos]
    if offset == 0:
        return grid_field
    if abs(offset) >= height:
        return jnp.zeros_like(grid_field)
    widths = [(0, 0)] * grid_field.ndim
    if offset > 0:
        kept_rows = lax.slice_in_dim(grid_field, offset, height, axis=axis_pos)
        widths[axis_pos] = (0, offset)
    else:
        kept_rows = lax.slice_in_dim(grid_field, 0, height + offset, axis=axis_pos)
        widths[axis_pos] = (-offset, 0)
    return jnp.pad(kept_rows, widths)


def gate_slope(pre_act):
    sigmoid_val = jax.nn.sigmoid(pre_act)
    return sigmoid_val * (1.0 + pre_act * (1.0 - sigmoid_val))


def reference(features, depth_w, point_w, point_bias, cotangent):
    dilations = (RATE_A, RATE_B)

    def one_image(totals, inputs):
        point_total, depth_total, bias_total = totals
        image_cells, upstream = inputs
        channels = image_cells.shape[2]
        outputs = point_w.shape[2]
        grad_field = jnp.zeros(image_cells.shape, jnp.float32)
        point_new = []
        depth_new = []
        bias_new = []
        for branch, dilation in enumerate(dilations):
            moved_taps = {}
            depth_acc = jnp.zeros(image_cells.shape, jnp.float32)
            for lon_step in (-1, 0, 1):
                rolled = jnp.roll(image_cells, -lon_step * dilation, axis=0)
                for lat_step in (-1, 0, 1):
                    tapped = lat_shift(rolled, lat_step * dilation, 1).astype(jnp.float32)
                    moved_taps[(lat_step, lon_step)] = tapped
                    depth_acc = depth_acc + depth_w[branch, lat_step + 1, lon_step + 1].astype(jnp.float32) * tapped
            depth_out = depth_acc.astype(jnp.bfloat16)
            flat_depth = depth_out.reshape(-1, channels)
            point_act = jnp.dot(flat_depth, point_w[branch], preferred_element_type=jnp.float32) + point_bias[branch]
            upstream_part = upstream[:, :, branch * outputs:(branch + 1) * outputs].reshape(-1, outputs).astype(jnp.float32)
            pgrad = (upstream_part * gate_slope(point_act)).astype(jnp.bfloat16)
            bias_new.append(bias_total[branch] + jnp.sum(pgrad.astype(jnp.float32), axis=0))
            point_new.append(point_total[branch] + jnp.dot(flat_depth.T, pgrad, preferred_element_type=jnp.float32))
            dgrad = jnp.dot(pgrad, point_w[branch].T, preferred_element_type=jnp.float32).astype(jnp.bfloat16)
            dgrad = dgrad.reshape(image_cells.shape)
            dgrad_wide = dgrad.astype(jnp.float32)
            tap_rows = []
            for lat_step in (-1, 0, 1):
                tap_cols = []
                for lon_step in (-1, 0, 1):
                    tap_cols.append(jnp.sum(moved_taps[(lat_step, lon_step)] * dgrad_wide, axis=(0, 1)))
                    behind = lat_shift(jnp.roll(dgrad, lon_step * dilation, axis=0), -lat_step * dilation, 1)
                    grad_field = grad_field + depth_w[branch, lat_step + 1, lon_step + 1].astype(jnp.float32) * behind.astype(jnp.float32)
                tap_rows.append(jnp.stack(tap_cols))
            depth_new.append(depth_total[branch] + jnp.stack(tap_rows))
        new_totals = (jnp.stack(point_new), jnp.stack(depth_new), jnp.stack(bias_new))
        return new_totals, grad_field.astype(jnp.bfloat16)

    start_totals = (jnp.zeros((2, C, C_OUT), jnp.float32), jnp.zeros((2, 3, 3, C), jnp.float32), jnp.zeros((2, C_OUT), jnp.float32))
    final_totals, feature_grad = lax.scan(one_image, start_totals, (features, cotangent))
    point_total, depth_total, bias_total = final_totals
    depth_grad = (depth_total / IMGS).astype(jnp.bfloat16)
    point_grad = (point_total / IMGS).astype(jnp.bfloat16)
    bias_grad = bias_total / IMGS
    return (feature_grad, depth_grad, point_grad, bias_grad)
```

```python
import functools

import jax
import jax.numpy as jnp
from jax import lax
from jax.experimental import pallas as pl
from jax.experimental.pallas import tpu as pltpu
from jax.sharding import PartitionSpec as P

MESH = pl.DeviceIdType.MESH
F32 = jnp.float32
BF16 = jnp.bfloat16

RATE_A = 24
RATE_B = 36


def from_behind(block, axis, distance):
    devices = range(lax.axis_size(axis))
    route = [((i - distance) % len(devices), i) for i in devices]
    return lax.ppermute(block, axis, route)


def lat_shift(grid_field, offset, axis_pos):
    height = grid_field.shape[axis_pos]
    if offset == 0:
        return grid_field
    widths = [(0, 0)] * grid_field.ndim
    if offset > 0:
        kept_rows = lax.slice_in_dim(grid_field, offset, height, axis=axis_pos)
        widths[axis_pos] = (0, offset)
    else:
        kept_rows = lax.slice_in_dim(grid_field, 0, height + offset, axis=axis_pos)
        widths[axis_pos] = (-offset, 0)
    return jnp.pad(kept_rows, widths)


def gate_slope(pre_act):
    sigmoid_val = jax.nn.sigmoid(pre_act)
    return sigmoid_val * (1.0 + pre_act * (1.0 - sigmoid_val))


def column_plan(dilation, direction, columns, group_size):
    run_list = []
    for column in range(columns):
        target = column + direction * dilation
        offset = target // columns
        local_col = target % columns
        if run_list and run_list[-1][0] == offset:
            run_list[-1][2] = local_col + 1
        else:
            run_list.append([offset, local_col, local_col + 1])
    return [(-entry[0] % group_size, entry[1], entry[2]) for entry in run_list]


def join_pieces(piece_list):
    if len(piece_list) == 1:
        return piece_list[0]
    return jnp.concatenate(piece_list, axis=1)


def fetch_each(grid_field, offset_pairs, group_size, send_fn):
    result = {}
    for offset_pair in offset_pairs:
        piece_list = []
        for shift_by, first_col, finish in column_plan(
            offset_pair[0], offset_pair[1], grid_field.shape[1], group_size
        ):
            column_piece = grid_field[:, first_col:finish]
            if shift_by != 0:
                column_piece = send_fn(column_piece, shift_by)
            piece_list.append(column_piece)
        result[offset_pair] = join_pieces(piece_list)
    return result


def send_features(column_piece, shift_by):
    return from_behind(column_piece, "lon", shift_by)


def send_grads(column_piece, shift_by):
    return from_behind(column_piece, "lon", shift_by)


def per_device(features, depth_w, point_w, point_bias, cotangent):
    group_size = lax.axis_size("lon")
    channels = features.shape[3]
    outputs = point_w.shape[2]
    dilations = (RATE_A, RATE_B)
    offset_pairs = [(dilation, direction) for dilation in dilations for direction in (-1, 1)]
    moved_in = fetch_each(features, offset_pairs, group_size, send_features)
    depth_outs = []
    for branch, dilation in enumerate(dilations):
        depth_acc = jnp.zeros(features.shape, jnp.float32)
        for lon_step in (-1, 0, 1):
            source = features if lon_step == 0 else moved_in[dilation, lon_step]
            for lat_step in (-1, 0, 1):
                tapped = lat_shift(source, lat_step * dilation, 2).astype(jnp.float32)
                depth_acc = (
                    depth_acc
                    + depth_w[branch, lat_step + 1, lon_step + 1].astype(jnp.float32) * tapped
                )
        depth_outs.append(depth_acc.astype(jnp.bfloat16))
    point_terms = []
    bias_terms = []
    dgrad_list = []
    for branch, dilation in enumerate(dilations):
        flat_depth = depth_outs[branch].reshape(-1, channels)
        point_act = (
            jnp.dot(flat_depth, point_w[branch], preferred_element_type=jnp.float32)
            + point_bias[branch]
        )
        upstream_part = (
            cotangent[..., branch * outputs : (branch + 1) * outputs]
            .reshape(-1, outputs)
            .astype(jnp.float32)
        )
        pgrad = (upstream_part * gate_slope(point_act)).astype(jnp.bfloat16)
        bias_terms.append(jnp.sum(pgrad.astype(jnp.float32), axis=0))
        point_terms.append(
            lax.dot_general(
                flat_depth, pgrad, (((0,), (0,)), ((), ())), preferred_element_type=jnp.float32
            )
        )
        dgrad = lax.dot_general(
            pgrad, point_w[branch], (((1,), (1,)), ((), ())), preferred_element_type=jnp.float32
        )
        dgrad_list.append(dgrad.astype(jnp.bfloat16).reshape(features.shape))
    point_local = jnp.stack(point_terms)
    bias_local = jnp.stack(bias_terms)
    grad_field = jnp.zeros(features.shape, jnp.float32)
    depth_terms = []
    for branch, dilation in enumerate(dilations):
        branch_pairs = [(dilation, -1), (dilation, 1)]
        moved_back = fetch_each(dgrad_list[branch], branch_pairs, group_size, send_grads)
        dgrad_wide = dgrad_list[branch].astype(jnp.float32)
        tap_rows = []
        for lat_step in (-1, 0, 1):
            tap_cols = []
            for lon_step in (-1, 0, 1):
                source = features if lon_step == 0 else moved_in[dilation, lon_step]
                tapped = lat_shift(source, lat_step * dilation, 2).astype(jnp.float32)
                tap_cols.append(jnp.sum(tapped * dgrad_wide, axis=(0, 1, 2)))
                behind = dgrad_list[branch] if lon_step == 0 else moved_back[dilation, -lon_step]
                behind = lat_shift(behind, -lat_step * dilation, 2).astype(jnp.float32)
                grad_field = (
                    grad_field
                    + depth_w[branch, lat_step + 1, lon_step + 1].astype(jnp.float32) * behind
                )
            tap_rows.append(jnp.stack(tap_cols))
        depth_terms.append(jnp.stack(tap_rows))
    depth_local = jnp.stack(depth_terms)
    feature_grad = grad_field.astype(jnp.bfloat16)
    point_sum, depth_sum, bias_sum = lax.psum((point_local, depth_local, bias_local), ("dp", "lon"))
    images = lax.axis_size("dp") * features.shape[0]
    depth_grad = (depth_sum / images).astype(jnp.bfloat16)
    point_grad = (point_sum / images).astype(jnp.bfloat16)
    bias_grad = bias_sum / images
    return (feature_grad, depth_grad, point_grad, bias_grad)


LANES = 128
CHUNK = 160
POINT_ROWS = 144
FIRST = 80


def ring(e, g):
    return (g + e) % 3


def widen(block):
    wide = block.astype(F32)
    return wide[0:24], wide[24:48]


def join_rows(low, high):
    return jnp.concatenate([low, high], axis=0)


def fold(block):
    total = block[0:8]
    for at in range(8, block.shape[0], 8):
        total = total + block[at : at + 8]
    return total


def edge_taps(wide):
    rows = lax.broadcasted_iota(jnp.int32, (16, LANES), 0)
    ahead = jnp.where(rows < 12, pltpu.roll(wide[32:48], 12, 0), 0.0)
    behind = jnp.where(rows >= 4, pltpu.roll(wide[0:16], 4, 0), 0.0)
    return ahead, behind


def taps_a(dw_ref, lanes):
    rows = [dw_ref[0, a, :, lanes].astype(F32) for a in range(3)]
    return [[rows[a][e : e + 1] for e in range(3)] for a in range(3)]


def taps_b(dw_ref, lanes):
    rows = [dw_ref[1, a, :, lanes].astype(F32) for a in range(3)]
    return [row[0:1] + row[1:2] + row[2:3] for row in rows]


def lane_block(at):
    return pl.ds(pl.multiple_of(at * LANES, LANES), LANES)


def point_step(depth, weight, bias, upstream):
    act = jnp.dot(depth, weight, preferred_element_type=F32) + bias
    return (upstream.astype(F32) * gate_slope(act)).astype(BF16)


def spread_back(pgrad_ref, pw_ref, branch, out_ref):
    @pl.loop(0, 3)
    def _(at):
        cols = pl.ds(pl.multiple_of(at * 384, 384), 384)
        out_ref[:, cols] = lax.dot_general(
            pgrad_ref[...], pw_ref[branch, cols, :], (((1,), (1,)), ((), ())), preferred_element_type=F32
        ).astype(BF16)


def point_terms(depth_ref, pgrad_ref, wide_ref, acc, half):
    @pl.loop(0, 3)
    def _(at):
        cols = pl.ds(pl.multiple_of(at * 384, 384), 384)
        wide_ref[cols, :] = lax.dot_general(
            depth_ref[:, cols], pgrad_ref[...], (((0,), (0,)), ((), ())), preferred_element_type=F32
        )

    @pl.loop(0, 4)
    def _(at):
        for upper in range(2):
            for side in range(2):
                start = pl.multiple_of((upper * 4 + at) * POINT_ROWS, 16)
                block = wide_ref[pl.ds(start, POINT_ROWS), side * LANES : (side + 1) * LANES]
                acc[half, side, upper, at, 0:POINT_ROWS, :] = block.astype(BF16)


def small_slot(at):
    return at // 8, (at // 4) % 2, at % 4


def small_terms(taps_ref, pgrad_ref, acc, half):
    for at in range(9):
        y, x, z = small_slot(at)
        block = taps_ref[:, at * LANES : (at + 1) * LANES]
        acc[half, y, x, z, POINT_ROWS:CHUNK, :] = block.astype(BF16)
    total = jnp.sum(pgrad_ref[...].astype(F32), axis=0, keepdims=True)
    for at in range(2):
        y, x, z = small_slot(9 + at)
        block = jnp.broadcast_to(total[:, at * LANES : (at + 1) * LANES], (16, LANES))
        acc[half, y, x, z, POINT_ROWS:CHUNK, :] = block.astype(BF16)
    for at in range(11, 16):
        y, x, z = small_slot(at)
        acc[half, y, x, z, POINT_ROWS:CHUNK, :] = jnp.zeros((16, LANES), BF16)


def whole_kernel(
    images, feat_ref, dw_ref, pw_ref, bias_ref, cot_ref,
    fgrad_ref, dgrad_out, pgrad_out, bgrad_out,
    feat_in, cot_in, pg_in, depth_s, pg_a, pg_b, dg_a, dg_b, wide_s, taps_s,
    acc, cur, fin, r0, r1y, r1x, r2y, r2x, r3, send_sem, recv_sem,
):
    dp = lax.axis_index("dp")
    my = lax.axis_index("lon")
    core = lax.rem(dp, 2)
    mx = lax.rem(dp // 2, 2)
    mz = dp // 4
    other_y = {"dp": dp, "lon": 1 - my}
    other_core = {"dp": dp + 1 - 2 * core, "lon": my}
    other_x = {"dp": dp + 2 - 4 * mx, "lon": my}
    other_z = [{"dp": lax.rem(dp + 4 * step, 16), "lon": my} for step in (1, 2, 3)]

    barrier = pltpu.get_barrier_semaphore()
    for peer in [other_y, other_core, other_x] + other_z:
        pl.semaphore_signal(barrier, inc=1, device_id=peer, device_id_type=MESH)
    pl.semaphore_wait(barrier, 6)

    def send(at, src, dst, peer):
        copy = pltpu.make_async_remote_copy(
            src_ref=src, dst_ref=dst, send_sem=send_sem.at[at], recv_sem=recv_sem.at[at],
            device_id=peer, device_id_type=MESH,
        )
        copy.start()
        return copy

    feat_copy = send(0, feat_ref.at[144:288], feat_in, other_y)
    cot_copy = send(1, cot_ref.at[144:288, 0:256], cot_in, other_y)

    @pl.loop(0, 9)
    def _(at):
        lanes = lane_block(at)
        w = taps_b(dw_ref, lanes)
        for col in range(9):
            rows = pl.ds(col * 48, 48)
            wide = feat_ref[rows, lanes].astype(F32)
            ahead, behind = edge_taps(wide)
            low = w[1] * wide[0:16] + w[2] * ahead
            high = w[1] * wide[32:48] + w[0] * behind
            depth = jnp.concatenate([low, w[1] * wide[16:32], high], axis=0)
            depth_s[rows, lanes] = depth.astype(BF16)

    pg_b[...] = point_step(depth_s[...], pw_ref[1], bias_ref[1:2, :], cot_ref[:, 256:512])
    point_terms(depth_s, pg_b, wide_s, acc, 1)
    spread_back(pg_b, pw_ref, 1, dg_b)

    taps_s[...] = jnp.zeros_like(taps_s)

    @pl.loop(0, 9)
    def _(at):
        lanes = lane_block(at)
        sums = [jnp.zeros((8, LANES), F32) for _ in range(3)]
        for col in range(9):
            rows = pl.ds(col * 48, 48)
            wide = feat_ref[rows, lanes].astype(F32)
            grad = dg_b[rows, lanes].astype(F32)
            ahead, behind = edge_taps(wide)
            sums[0] = sums[0] + fold(behind * grad[32:48])
            sums[1] = sums[1] + fold(wide * grad)
            sums[2] = sums[2] + fold(ahead * grad[0:16])
        for a in range(3):
            total = jnp.sum(sums[a], axis=0, keepdims=True)
            taps_s[3 * a : 3 * a + 3, lanes] = jnp.broadcast_to(total, (3, LANES))

    small_terms(taps_s, pg_b, acc, 1)

    feat_copy.wait()
    cot_copy.wait()

    def cell_rows(g, t):
        return pl.ds((3 * g + t) * 48, 48)

    def load_feat(g, t, lanes):
        if g == 2:
            return widen(feat_in[pl.ds(t * 48, 48), lanes])
        return widen(feat_ref[pl.ds((6 * g + t) * 48, 48), lanes])

    @pl.loop(0, 9)
    def _(at):
        lanes = lane_block(at)
        w = taps_a(dw_ref, lanes)
        for t in range(3):
            cells = [load_feat(g, t, lanes) for g in range(3)]
            for g in range(3):
                low = high = 0.0
                for e in (-1, 0, 1):
                    src_low, src_high = cells[ring(e, g)]
                    low = low + w[1][e + 1] * src_low + w[2][e + 1] * src_high
                    high = high + w[1][e + 1] * src_high + w[0][e + 1] * src_low
                depth_s[cell_rows(g, t), lanes] = join_rows(low, high).astype(BF16)

    for g in range(3):
        rows = pl.ds(144 * g, 144)
        upstream = cot_in[...] if g == 2 else cot_ref[pl.ds(288 * g, 144), 0:256]
        pg_a[rows, :] = point_step(depth_s[rows, :], pw_ref[0], bias_ref[0:1, :], upstream)
    pg_copy = send(2, pg_a, pg_in, other_y)
    point_terms(depth_s, pg_a, wide_s, acc, 0)
    spread_back(pg_a, pw_ref, 0, dg_a)

    @pl.loop(0, 9)
    def _(at):
        lanes = lane_block(at)
        sums = [[jnp.zeros((8, LANES), F32) for _ in range(3)] for _ in range(3)]
        for t in range(3):
            cells = [load_feat(g, t, lanes) for g in range(3)]
            for g in range(3):
                grad_low, grad_high = widen(dg_a[cell_rows(g, t), lanes])
                for e in (-1, 0, 1):
                    src_low, src_high = cells[ring(e, g)]
                    sums[0][e + 1] = sums[0][e + 1] + fold(src_low * grad_high)
                    sums[1][e + 1] = sums[1][e + 1] + fold(src_low * grad_low + src_high * grad_high)
                    sums[2][e + 1] = sums[2][e + 1] + fold(src_high * grad_low)
        for a in range(3):
            for e in range(3):
                taps_s[3 * a + e : 3 * a + e + 1, lanes] = jnp.sum(sums[a][e], axis=0, keepdims=True)

    small_terms(taps_s, pg_a, acc, 0)
    sib_copy = send(3, acc.at[1 - core], r0, other_core)

    def branch_b_grad(rows, lanes, w):
        grad = dg_b[rows, lanes].astype(F32)
        ahead, behind = edge_taps(grad)
        low = w[1] * grad[0:16] + w[0] * ahead
        high = w[1] * grad[32:48] + w[2] * behind
        return jnp.concatenate([low, w[1] * grad[16:32], high], axis=0)

    def branch_a_grad(w, grads, g):
        low = high = 0.0
        for e in (-1, 0, 1):
            src_low, src_high = grads[ring(-e, g)]
            low = low + w[1][e + 1] * src_low + w[0][e + 1] * src_high
            high = high + w[1][e + 1] * src_high + w[2][e + 1] * src_low
        return join_rows(low, high)

    @pl.loop(0, 9)
    def _(at):
        lanes = lane_block(at)
        w = taps_a(dw_ref, lanes)
        wb = taps_b(dw_ref, lanes)
        for t in range(3):
            grads = [widen(dg_a[cell_rows(g, t), lanes]) for g in range(3)]
            for g in range(2):
                rows = pl.ds((6 * g + t) * 48, 48)
                total = branch_a_grad(w, grads, g) + branch_b_grad(rows, lanes, wb)
                fgrad_ref[rows, lanes] = total.astype(BF16)

    sib_copy.wait()

    @pl.loop(0, 4)
    def _(z):
        for y in range(2):
            for x in range(2):
                cur[y, x, z] = (acc[core, y, x, z].astype(F32) + r0[y, x, z].astype(F32)).astype(BF16)

    rows_y = pl.ds(0, FIRST)
    rows_x = pl.ds(FIRST, CHUNK - FIRST)
    one_y = send(4, cur.at[1 - my, :, :, rows_y], r1y, other_y)
    one_x = send(5, cur.at[:, 1 - mx, :, rows_x], r1x, other_x)

    pg_copy.wait()
    spread_back(pg_in, pw_ref, 0, dg_a)

    @pl.loop(0, 9)
    def _(at):
        lanes = lane_block(at)
        w = taps_a(dw_ref, lanes)
        wb = taps_b(dw_ref, lanes)
        for t in range(3):
            grads = [widen(dg_a[cell_rows(g, t), lanes]) for g in range(3)]
            rows = pl.ds((3 + t) * 48, 48)
            total = branch_a_grad(w, grads, 2) + branch_b_grad(rows, lanes, wb)
            fgrad_ref[rows, lanes] = total.astype(BF16)

    one_y.wait()
    one_x.wait()

    def add_into(at, extra):
        cur[at] = (cur[at].astype(F32) + extra.astype(F32)).astype(BF16)

    @pl.loop(0, 4)
    def _(z):
        for k in range(2):
            add_into((my, k, z, rows_y), r1y[k, z])
            add_into((k, mx, z, rows_x), r1x[k, z])

    two_x = send(6, cur.at[my, 1 - mx, :, rows_y], r2x, other_x)
    two_y = send(7, cur.at[1 - my, mx, :, rows_x], r2y, other_y)
    two_x.wait()
    two_y.wait()

    @pl.loop(0, 4)
    def _(z):
        add_into((my, mx, z, rows_y), r2x[z])
        add_into((my, mx, z, rows_x), r2y[z])

    three = [
        send(8 + k, cur.at[my, mx, lax.rem(mz + k + 1, 4)], r3.at[k], other_z[k]) for k in range(3)
    ]
    for copy in three:
        copy.wait()
    total = cur[my, mx, mz].astype(F32)
    for k in range(3):
        total = total + r3[k].astype(F32)
    fin[core, my, mx, mz] = (total * (1.0 / images)).astype(BF16)

    def share(at, index, peer):
        return send(at, fin.at[index], fin.at[index], peer)

    for copy in [share(11 + k, (core, my, mx, mz), other_z[k]) for k in range(3)]:
        copy.wait()
    every = slice(None)
    five = [
        share(14, (core, my, mx, every, rows_y), other_x),
        share(15, (core, my, mx, every, rows_x), other_y),
    ]
    for copy in five:
        copy.wait()
    six = [
        share(16, (core, my, every, every, rows_y), other_y),
        share(17, (core, every, mx, every, rows_x), other_x),
    ]
    for copy in six:
        copy.wait()
    share(18, (core,), other_core).wait()

    for half in range(2):
        @pl.loop(0, 4)
        def _(at):
            for upper in range(2):
                for side in range(2):
                    start = pl.multiple_of((upper * 4 + at) * POINT_ROWS, 16)
                    block = fin[half, side, upper, at, 0:POINT_ROWS, :]
                    pgrad_out[half, pl.ds(start, POINT_ROWS), side * LANES : (side + 1) * LANES] = block

        for at in range(9):
            y, x, z = small_slot(at)
            block = fin[half, y, x, z, POINT_ROWS:CHUNK, :].astype(F32)
            for a in range(3):
                part = block[3 * a : 3 * a + 3].astype(BF16)
                dgrad_out[half, a, :, at * LANES : (at + 1) * LANES] = part
        for at in range(2):
            y, x, z = small_slot(9 + at)
            block = fin[half, y, x, z, POINT_ROWS:CHUNK, :].astype(F32)
            bgrad_out[half : half + 1, at * LANES : (at + 1) * LANES] = block[0:1]


def fused_step(features, depth_w, point_w, point_bias, cotangent):
    images = lax.axis_size("dp") * features.shape[0]
    cells, channels, outputs = 432, features.shape[3], point_w.shape[2]
    scratch = [
        pltpu.VMEM((144, channels), BF16),
        pltpu.VMEM((144, outputs), BF16),
        pltpu.VMEM((cells, outputs), BF16),
        pltpu.VMEM((cells, channels), BF16),
        pltpu.VMEM((cells, outputs), BF16),
        pltpu.VMEM((cells, outputs), BF16),
        pltpu.VMEM((cells, channels), BF16),
        pltpu.VMEM((cells, channels), BF16),
        pltpu.VMEM((channels, outputs), F32),
        pltpu.VMEM((16, channels), F32),
        pltpu.VMEM((2, 2, 2, 4, CHUNK, LANES), BF16),
        pltpu.VMEM((2, 2, 4, CHUNK, LANES), BF16),
        pltpu.VMEM((2, 2, 2, 4, CHUNK, LANES), BF16),
        pltpu.VMEM((2, 2, 4, CHUNK, LANES), BF16),
        pltpu.VMEM((2, 4, FIRST, LANES), BF16),
        pltpu.VMEM((2, 4, FIRST, LANES), BF16),
        pltpu.VMEM((4, FIRST, LANES), BF16),
        pltpu.VMEM((4, FIRST, LANES), BF16),
        pltpu.VMEM((3, CHUNK, LANES), BF16),
        pltpu.SemaphoreType.DMA((19,)),
        pltpu.SemaphoreType.DMA((19,)),
    ]
    in_vmem = pl.BlockSpec(memory_space=pltpu.VMEM)
    feature_grad, depth_grad, point_grad, bias_grad = pl.pallas_call(
        functools.partial(whole_kernel, images),
        out_shape=(
            jax.ShapeDtypeStruct((cells, channels), BF16),
            jax.ShapeDtypeStruct(depth_w.shape, BF16),
            jax.ShapeDtypeStruct(point_w.shape, BF16),
            jax.ShapeDtypeStruct(point_bias.shape, F32),
        ),
        in_specs=[in_vmem] * 5,
        out_specs=[in_vmem] * 4,
        scratch_shapes=scratch,
        compiler_params=pltpu.CompilerParams(
            collective_id=0, has_side_effects=True, vmem_limit_bytes=40 * 1024 * 1024
        ),
        cost_estimate=pl.CostEstimate(flops=2 * 7 * cells * channels * outputs, bytes_accessed=8000000, transcendentals=0),
    )(features.reshape(cells, channels), depth_w, point_w, point_bias, cotangent.reshape(cells, 2 * outputs))
    return feature_grad.reshape(features.shape), depth_grad, point_grad, bias_grad


def fits_fused(mesh):
    return dict(mesh.shape) == {"dp": 16, "lon": 2}


def chosen_step(mesh):
    def step(features, depth_w, point_w, point_bias, cotangent):
        arguments = (features, depth_w, point_w, point_bias, cotangent)
        if fits_fused(mesh) and features.shape == (1, 9, 48, 1152) and point_w.shape[2] == 256:
            return fused_step(*arguments)
        return per_device(*arguments)

    return step


def solution(mesh):
    placed = (P("dp", "lon", None, None), P(), P(), P(), P("dp", "lon", None, None))
    return jax.shard_map(
        chosen_step(mesh),
        mesh=mesh,
        in_specs=placed,
        out_specs=(P("dp", "lon", None, None), P(), P(), P()),
        check_vma=False,
    )
```

```python
import functools

import jax
import jax.numpy as jnp
from jax import lax
from jax.experimental import pallas as pl
from jax.experimental.pallas import tpu as pltpu
from jax.sharding import PartitionSpec as P

MESH = pl.DeviceIdType.MESH
F32 = jnp.float32
BF16 = jnp.bfloat16

RATE_A = 24
RATE_B = 36


def from_behind(block, axis, distance):
    devices = range(lax.axis_size(axis))
    route = [((i - distance) % len(devices), i) for i in devices]
    return lax.ppermute(block, axis, route)


def lat_shift(grid_field, offset, axis_pos):
    height = grid_field.shape[axis_pos]
    if offset == 0:
        return grid_field
    widths = [(0, 0)] * grid_field.ndim
    if offset > 0:
        kept_rows = lax.slice_in_dim(grid_field, offset, height, axis=axis_pos)
        widths[axis_pos] = (0, offset)
    else:
        kept_rows = lax.slice_in_dim(grid_field, 0, height + offset, axis=axis_pos)
        widths[axis_pos] = (-offset, 0)
    return jnp.pad(kept_rows, widths)


def gate_slope(pre_act):
    sigmoid_val = jax.nn.sigmoid(pre_act)
    return sigmoid_val * (1.0 + pre_act * (1.0 - sigmoid_val))


def column_plan(dilation, direction, columns, group_size):
    run_list = []
    for column in range(columns):
        target = column + direction * dilation
        offset = target // columns
        local_col = target % columns
        if run_list and run_list[-1][0] == offset:
            run_list[-1][2] = local_col + 1
        else:
            run_list.append([offset, local_col, local_col + 1])
    return [(-entry[0] % group_size, entry[1], entry[2]) for entry in run_list]


def join_pieces(piece_list):
    if len(piece_list) == 1:
        return piece_list[0]
    return jnp.concatenate(piece_list, axis=1)


def fetch_each(grid_field, offset_pairs, group_size, send_fn):
    result = {}
    for offset_pair in offset_pairs:
        piece_list = []
        for shift_by, first_col, finish in column_plan(
            offset_pair[0], offset_pair[1], grid_field.shape[1], group_size
        ):
            column_piece = grid_field[:, first_col:finish]
            if shift_by != 0:
                column_piece = send_fn(column_piece, shift_by)
            piece_list.append(column_piece)
        result[offset_pair] = join_pieces(piece_list)
    return result


def send_features(column_piece, shift_by):
    return from_behind(column_piece, "lon", shift_by)


def send_grads(column_piece, shift_by):
    return from_behind(column_piece, "lon", shift_by)


def per_device(features, depth_w, point_w, point_bias, cotangent):
    group_size = lax.axis_size("lon")
    channels = features.shape[3]
    outputs = point_w.shape[2]
    dilations = (RATE_A, RATE_B)
    offset_pairs = [(dilation, direction) for dilation in dilations for direction in (-1, 1)]
    moved_in = fetch_each(features, offset_pairs, group_size, send_features)
    depth_outs = []
    for branch, dilation in enumerate(dilations):
        depth_acc = jnp.zeros(features.shape, jnp.float32)
        for lon_step in (-1, 0, 1):
            source = features if lon_step == 0 else moved_in[dilation, lon_step]
            for lat_step in (-1, 0, 1):
                tapped = lat_shift(source, lat_step * dilation, 2).astype(jnp.float32)
                depth_acc = (
                    depth_acc
                    + depth_w[branch, lat_step + 1, lon_step + 1].astype(jnp.float32) * tapped
                )
        depth_outs.append(depth_acc.astype(jnp.bfloat16))
    point_terms = []
    bias_terms = []
    dgrad_list = []
    for branch, dilation in enumerate(dilations):
        flat_depth = depth_outs[branch].reshape(-1, channels)
        point_act = (
            jnp.dot(flat_depth, point_w[branch], preferred_element_type=jnp.float32)
            + point_bias[branch]
        )
        upstream_part = (
            cotangent[..., branch * outputs : (branch + 1) * outputs]
            .reshape(-1, outputs)
            .astype(jnp.float32)
        )
        pgrad = (upstream_part * gate_slope(point_act)).astype(jnp.bfloat16)
        bias_terms.append(jnp.sum(pgrad.astype(jnp.float32), axis=0))
        point_terms.append(
            lax.dot_general(
                flat_depth, pgrad, (((0,), (0,)), ((), ())), preferred_element_type=jnp.float32
            )
        )
        dgrad = lax.dot_general(
            pgrad, point_w[branch], (((1,), (1,)), ((), ())), preferred_element_type=jnp.float32
        )
        dgrad_list.append(dgrad.astype(jnp.bfloat16).reshape(features.shape))
    point_local = jnp.stack(point_terms)
    bias_local = jnp.stack(bias_terms)
    grad_field = jnp.zeros(features.shape, jnp.float32)
    depth_terms = []
    for branch, dilation in enumerate(dilations):
        branch_pairs = [(dilation, -1), (dilation, 1)]
        moved_back = fetch_each(dgrad_list[branch], branch_pairs, group_size, send_grads)
        dgrad_wide = dgrad_list[branch].astype(jnp.float32)
        tap_rows = []
        for lat_step in (-1, 0, 1):
            tap_cols = []
            for lon_step in (-1, 0, 1):
                source = features if lon_step == 0 else moved_in[dilation, lon_step]
                tapped = lat_shift(source, lat_step * dilation, 2).astype(jnp.float32)
                tap_cols.append(jnp.sum(tapped * dgrad_wide, axis=(0, 1, 2)))
                behind = dgrad_list[branch] if lon_step == 0 else moved_back[dilation, -lon_step]
                behind = lat_shift(behind, -lat_step * dilation, 2).astype(jnp.float32)
                grad_field = (
                    grad_field
                    + depth_w[branch, lat_step + 1, lon_step + 1].astype(jnp.float32) * behind
                )
            tap_rows.append(jnp.stack(tap_cols))
        depth_terms.append(jnp.stack(tap_rows))
    depth_local = jnp.stack(depth_terms)
    feature_grad = grad_field.astype(jnp.bfloat16)
    point_sum, depth_sum, bias_sum = lax.psum((point_local, depth_local, bias_local), ("dp", "lon"))
    images = lax.axis_size("dp") * features.shape[0]
    depth_grad = (depth_sum / images).astype(jnp.bfloat16)
    point_grad = (point_sum / images).astype(jnp.bfloat16)
    bias_grad = bias_sum / images
    return (feature_grad, depth_grad, point_grad, bias_grad)


LANES = 128
CHUNK = 80
POINT_ROWS = 72
BULK = 64
SENDS = 33


def ring(e, g):
    return (g + e) % 3


def widen(block):
    wide = block.astype(F32)
    return wide[0:24], wide[24:48]


def join_rows(low, high):
    return jnp.concatenate([low, high], axis=0)


def fold(block):
    total = block[0:8]
    for at in range(8, block.shape[0], 8):
        total = total + block[at : at + 8]
    return total


def edge_taps(wide):
    rows = lax.broadcasted_iota(jnp.int32, (16, LANES), 0)
    ahead = jnp.where(rows < 12, pltpu.roll(wide[32:48], 12, 0), 0.0)
    behind = jnp.where(rows >= 4, pltpu.roll(wide[0:16], 4, 0), 0.0)
    return ahead, behind


def tap_row(dw_ref, branch, a, e, lanes):
    return dw_ref[a, e, :, lanes].astype(F32)[branch : branch + 1]


def taps_a(dw_ref, lanes):
    return [[tap_row(dw_ref, 0, a, e, lanes) for e in range(3)] for a in range(3)]


def taps_b(dw_ref, lanes):
    rows = [[tap_row(dw_ref, 1, a, e, lanes) for e in range(3)] for a in range(3)]
    return [row[0] + row[1] + row[2] for row in rows]


def lane_block(at):
    return pl.ds(pl.multiple_of(at * LANES, LANES), LANES)


def point_step(depth, weight, bias, upstream):
    act = jnp.dot(depth, weight, preferred_element_type=F32) + bias
    return (upstream.astype(F32) * gate_slope(act)).astype(BF16)


def spread_back(pgrad_ref, pw_ref, branch, out_ref):
    @pl.loop(0, 3)
    def _(at):
        cols = pl.ds(pl.multiple_of(at * 384, 384), 384)
        out_ref[:, cols] = lax.dot_general(
            pgrad_ref[...], pw_ref[branch, cols, :], (((1,), (1,)), ((), ())), preferred_element_type=F32
        ).astype(BF16)


def place(at):
    return at // 8, lax.rem(at // 4, 2), lax.rem(at, 4)


def point_terms(depth_ref, pgrad_ref, wide_ref, acc, branch):
    @pl.loop(0, 3)
    def _(at):
        cols = pl.ds(pl.multiple_of(at * 384, 384), 384)
        wide_ref[cols, :] = lax.dot_general(
            depth_ref[:, cols], pgrad_ref[...], (((0,), (0,)), ((), ())), preferred_element_type=F32
        )

    @pl.loop(0, 16)
    def _(at):
        y, x, z = place(at)
        rows = pl.ds(pl.multiple_of(at * POINT_ROWS, 8), BULK)
        for side in range(2):
            block = wide_ref[rows, side * LANES : (side + 1) * LANES]
            acc[branch, side, y, x, z, 0:BULK, :] = block.astype(BF16)


def small_terms(wide_ref, taps_ref, pgrad_ref, acc, branch):
    total = jnp.sum(pgrad_ref[...].astype(F32), axis=0, keepdims=True)
    for at in range(2):
        taps_ref[1, 9 + at, 0:1, :] = total[:, at * LANES : (at + 1) * LANES]

    @pl.loop(0, 16)
    def _(at):
        y, x, z = place(at)
        rows = pl.ds(pl.multiple_of(at * POINT_ROWS + BULK, 8), POINT_ROWS - BULK)
        for side in range(2):
            block = wide_ref[rows, side * LANES : (side + 1) * LANES]
            block = jnp.concatenate([block, taps_ref[side, at]], axis=0)
            acc[branch, side, y, x, z, BULK:CHUNK, :] = block.astype(BF16)


def store_results(fin, branch, pgrad_out, bgrad_out):
    @pl.loop(0, 8)
    def _(pair):
        y, x, z = place(pair * 2)
        rows = pl.ds(pl.multiple_of(pair * 2 * POINT_ROWS, 16), 2 * POINT_ROWS)
        for side in range(2):
            blocks = [fin[branch, side, y, x, z + k].astype(F32)[0:POINT_ROWS] for k in range(2)]
            pgrad_out[branch, rows, side * LANES : (side + 1) * LANES] = jnp.concatenate(blocks, axis=0).astype(BF16)

    for at in range(2):
        block = fin[branch, 1, 1, 0, 1 + at, BULK:CHUNK, :].astype(F32)
        bgrad_out[branch : branch + 1, at * LANES : (at + 1) * LANES] = block[8:9]


def store_taps(fin, dgrad_out):
    for at in range(9):
        lanes = slice(at * LANES, (at + 1) * LANES)
        y, x, z = at // 8, (at // 4) % 2, at % 4
        blocks = [
            [fin[branch, side, y, x, z, BULK:CHUNK, :].astype(F32)[8:16] for side in range(2)] for branch in range(2)
        ]
        for tap in range(9):
            side, row = tap // 8, tap % 8
            pair = [blocks[branch][side][row : row + 1] for branch in range(2)]
            dgrad_out[tap // 3, tap % 3, :, lanes] = jnp.concatenate(pair, axis=0).astype(BF16)


def whole_kernel(
    images, feat_hbm, dw_hbm, pw_hbm, bias_hbm, cot_hbm,
    fgrad_hbm, dgrad_hbm, pgrad_hbm, bgrad_hbm,
    fgrad_ref, dgrad_out, pgrad_out, bgrad_out,
    feat_ref, dw_ref, pw_ref, bias_ref, cot_ref,
    feat_in, cot_in, pg_in, depth_s, pg_a, pg_b, dg_a, dg_b, wide_s, taps_s,
    acc, cur, fin, r0, bx, bz, by, a1y, a1x, a2x, a2y, a3, load_sem, store_sem, send_sem, recv_sem,
):
    dp = lax.axis_index("dp")
    my = lax.axis_index("lon")
    core = lax.rem(dp, 2)
    mx = lax.rem(dp // 2, 2)
    mz = dp // 4
    other_y = {"dp": dp, "lon": 1 - my}
    other_core = {"dp": dp + 1 - 2 * core, "lon": my}
    other_x = {"dp": dp + 2 - 4 * mx, "lon": my}
    other_z = [{"dp": lax.rem(dp + 4 * step, 16), "lon": my} for step in (1, 2, 3)]

    loads = [
        pltpu.make_async_copy(src, dst, load_sem.at[at])
        for at, (src, dst) in enumerate(
            [(feat_hbm, feat_ref), (dw_hbm, dw_ref), (pw_hbm, pw_ref), (bias_hbm, bias_ref), (cot_hbm, cot_ref)]
        )
    ]
    for copy in loads:
        copy.start()

    barrier = pltpu.get_barrier_semaphore()
    for peer in [other_y, other_core, other_x] + other_z:
        pl.semaphore_signal(barrier, inc=1, device_id=peer, device_id_type=MESH)
    pl.semaphore_wait(barrier, 6)

    numbers = iter(range(SENDS))

    def send(src, dst, peer):
        at = next(numbers)
        copy = pltpu.make_async_remote_copy(
            src_ref=src, dst_ref=dst, send_sem=send_sem.at[at], recv_sem=recv_sem.at[at],
            device_id=peer, device_id_type=MESH,
        )
        copy.start()
        return copy

    stores = []

    def store(src, dst):
        copy = pltpu.make_async_copy(src, dst, store_sem.at[len(stores)])
        copy.start()
        stores.append(copy)

    def finish(copies):
        for copy in copies:
            copy.wait()

    feat_copy = send(feat_hbm.at[144:288], feat_in, other_y)
    cot_copy = send(cot_hbm.at[144:288, 0:256], cot_in, other_y)
    finish(loads)
    taps_s[...] = jnp.zeros_like(taps_s)

    def add_into(at, extra):
        cur[at] = (cur[at].astype(F32) + extra.astype(F32)).astype(BF16)

    def share(index, peer):
        return send(fin.at[index], fin.at[index], peer)

    def send_half(branch, rows):
        return send(acc.at[branch, 1 - core, :, :, :, rows], r0.at[branch, :, :, :, rows], other_core)

    def add_halves(branch):
        @pl.loop(0, 4)
        def _(z):
            for y in range(2):
                for x in range(2):
                    total = acc[branch, core, y, x, z].astype(F32) + r0[branch, y, x, z].astype(F32)
                    cur[branch, y, x, z] = total.astype(BF16)

    def settle(branch, extras):
        total = cur[branch, my, mx, mz].astype(F32)
        for extra in extras:
            total = total + extra.astype(F32)
        fin[branch, core, my, mx, mz] = (total * (1.0 / images)).astype(BF16)

    every = slice(None)
    lower, upper = pl.ds(0, 2), pl.ds(2, 2)

    @pl.loop(0, 9)
    def _(at):
        lanes = lane_block(at)
        w = taps_b(dw_ref, lanes)
        for col in range(9):
            rows = pl.ds(col * 48, 48)
            wide = feat_ref[rows, lanes].astype(F32)
            ahead, behind = edge_taps(wide)
            low = w[1] * wide[0:16] + w[2] * ahead
            high = w[1] * wide[32:48] + w[0] * behind
            depth = jnp.concatenate([low, w[1] * wide[16:32], high], axis=0)
            depth_s[rows, lanes] = depth.astype(BF16)

    pg_b[...] = point_step(depth_s[...], pw_ref[1], bias_ref[1:2, :], cot_ref[:, 256:512])
    point_terms(depth_s, pg_b, wide_s, acc, 1)
    b_step = [send_half(1, pl.ds(0, BULK))]
    spread_back(pg_b, pw_ref, 1, dg_b)

    @pl.loop(0, 9)
    def _(at):
        lanes = lane_block(at)
        sums = [jnp.zeros((8, LANES), F32) for _ in range(3)]
        for col in range(9):
            rows = pl.ds(col * 48, 48)
            wide = feat_ref[rows, lanes].astype(F32)
            grad = dg_b[rows, lanes].astype(F32)
            ahead, behind = edge_taps(wide)
            sums[0] = sums[0] + fold(behind * grad[32:48])
            sums[1] = sums[1] + fold(wide * grad)
            sums[2] = sums[2] + fold(ahead * grad[0:16])
        for a in range(3):
            total = jnp.sum(sums[a], axis=0, keepdims=True)
            for e in range(3):
                tap = 3 * a + e
                taps_s[tap // 8, at, tap % 8 : tap % 8 + 1, :] = total

    small_terms(wide_s, taps_s, pg_b, acc, 1)
    b_step.append(send_half(1, pl.ds(BULK, CHUNK - BULK)))
    finish(b_step)
    add_halves(1)
    b_step = [send(cur.at[1, :, 1 - mx], bx, other_x)]

    feat_copy.wait()
    cot_copy.wait()

    def cell_rows(g, t):
        return pl.ds((3 * g + t) * 48, 48)

    def load_feat(g, t, lanes):
        if g == 2:
            return widen(feat_in[pl.ds(t * 48, 48), lanes])
        return widen(feat_ref[pl.ds((6 * g + t) * 48, 48), lanes])

    @pl.loop(0, 9)
    def _(at):
        lanes = lane_block(at)
        w = taps_a(dw_ref, lanes)
        for t in range(3):
            cells = [load_feat(g, t, lanes) for g in range(3)]
            for g in range(3):
                low = high = 0.0
                for e in (-1, 0, 1):
                    src_low, src_high = cells[ring(e, g)]
                    low = low + w[1][e + 1] * src_low + w[2][e + 1] * src_high
                    high = high + w[1][e + 1] * src_high + w[0][e + 1] * src_low
                depth_s[cell_rows(g, t), lanes] = join_rows(low, high).astype(BF16)

    for g in range(3):
        rows = pl.ds(144 * g, 144)
        upstream = cot_in[...] if g == 2 else cot_ref[pl.ds(288 * g, 144), 0:256]
        pg_a[rows, :] = point_step(depth_s[rows, :], pw_ref[0], bias_ref[0:1, :], upstream)
    pg_copy = send(pg_a, pg_in, other_y)

    finish(b_step)

    @pl.loop(0, 4)
    def _(z):
        for y in range(2):
            add_into((1, y, mx, z), bx[y, z])

    b_step = [send(cur.at[1, :, mx, lax.rem(mz + k + 1, 4)], bz.at[k], other_z[k]) for k in range(3)]

    point_terms(depth_s, pg_a, wide_s, acc, 0)
    a_step = [send_half(0, pl.ds(0, BULK))]
    spread_back(pg_a, pw_ref, 0, dg_a)

    @pl.loop(0, 9)
    def _(at):
        lanes = lane_block(at)
        sums = [[jnp.zeros((8, LANES), F32) for _ in range(3)] for _ in range(3)]
        for t in range(3):
            cells = [load_feat(g, t, lanes) for g in range(3)]
            for g in range(3):
                grad_low, grad_high = widen(dg_a[cell_rows(g, t), lanes])
                for e in (-1, 0, 1):
                    src_low, src_high = cells[ring(e, g)]
                    sums[0][e + 1] = sums[0][e + 1] + fold(src_low * grad_high)
                    sums[1][e + 1] = sums[1][e + 1] + fold(src_low * grad_low + src_high * grad_high)
                    sums[2][e + 1] = sums[2][e + 1] + fold(src_high * grad_low)
        for a in range(3):
            for e in range(3):
                tap = 3 * a + e
                taps_s[tap // 8, at, tap % 8 : tap % 8 + 1, :] = jnp.sum(sums[a][e], axis=0, keepdims=True)

    small_terms(wide_s, taps_s, pg_a, acc, 0)
    a_step.append(send_half(0, pl.ds(BULK, CHUNK - BULK)))

    finish(b_step)
    for y in range(2):
        total = cur[1, y, mx, mz].astype(F32)
        for k in range(3):
            total = total + bz[k, y].astype(F32)
        cur[1, y, mx, mz] = total.astype(BF16)
    b_step = [send(cur.at[1, 1 - my, mx, mz], by, other_y)]

    finish(a_step)
    add_halves(0)
    a_step = [
        send(cur.at[0, 1 - my, :, lower], a1y, other_y),
        send(cur.at[0, :, 1 - mx, upper], a1x, other_x),
    ]

    finish(b_step)
    settle(1, [by[...]])
    b_step = [share((1, core, my, mx, mz), other_y)]

    def branch_b_grad(rows, lanes, w):
        grad = dg_b[rows, lanes].astype(F32)
        ahead, behind = edge_taps(grad)
        low = w[1] * grad[0:16] + w[0] * ahead
        high = w[1] * grad[32:48] + w[2] * behind
        return jnp.concatenate([low, w[1] * grad[16:32], high], axis=0)

    def branch_a_grad(w, grads, g):
        low = high = 0.0
        for e in (-1, 0, 1):
            src_low, src_high = grads[ring(-e, g)]
            low = low + w[1][e + 1] * src_low + w[0][e + 1] * src_high
            high = high + w[1][e + 1] * src_high + w[2][e + 1] * src_low
        return join_rows(low, high)

    @pl.loop(0, 9)
    def _(at):
        lanes = lane_block(at)
        w = taps_a(dw_ref, lanes)
        wb = taps_b(dw_ref, lanes)
        for t in range(3):
            grads = [widen(dg_a[cell_rows(g, t), lanes]) for g in range(3)]
            for g in range(2):
                rows = pl.ds((6 * g + t) * 48, 48)
                total = branch_a_grad(w, grads, g) + branch_b_grad(rows, lanes, wb)
                fgrad_ref[rows, lanes] = total.astype(BF16)

    finish(b_step)
    b_step = [share((1, core, every, mx, mz), peer) for peer in other_z]

    finish(a_step)
    for k in range(2):
        for z in range(2):
            add_into((0, my, k, z), a1y[k, z])
            add_into((0, k, mx, 2 + z), a1x[k, z])
    a_step = [
        send(cur.at[0, my, 1 - mx, lower], a2x, other_x),
        send(cur.at[0, 1 - my, mx, upper], a2y, other_y),
    ]

    pg_copy.wait()
    spread_back(pg_in, pw_ref, 0, dg_a)

    @pl.loop(0, 9)
    def _(at):
        lanes = lane_block(at)
        w = taps_a(dw_ref, lanes)
        wb = taps_b(dw_ref, lanes)
        for t in range(3):
            grads = [widen(dg_a[cell_rows(g, t), lanes]) for g in range(3)]
            rows = pl.ds((3 + t) * 48, 48)
            total = branch_a_grad(w, grads, 2) + branch_b_grad(rows, lanes, wb)
            fgrad_ref[rows, lanes] = total.astype(BF16)

    store(fgrad_ref, fgrad_hbm)

    finish(a_step)
    for z in range(2):
        add_into((0, my, mx, z), a2x[z])
        add_into((0, my, mx, 2 + z), a2y[z])
    a_step = [send(cur.at[0, my, mx, lax.rem(mz + k + 1, 4)], a3.at[k], other_z[k]) for k in range(3)]

    finish(b_step)
    b_step = [share((1, core, every, mx), other_x)]

    finish(a_step)
    settle(0, [a3[k] for k in range(3)])
    a_step = [share((0, core, my, mx, mz), peer) for peer in other_z]

    finish(b_step)
    b_step = [share((1, core), other_core)]

    finish(a_step)
    a_step = [
        share((0, core, my, mx, lower), other_x),
        share((0, core, my, mx, upper), other_y),
    ]

    finish(b_step)
    store_results(fin, 1, pgrad_out, bgrad_out)
    store(pgrad_out.at[1], pgrad_hbm.at[1])

    finish(a_step)
    a_step = [
        share((0, core, my, every, lower), other_y),
        share((0, core, every, mx, upper), other_x),
    ]
    finish(a_step)
    finish([share((0, core), other_core)])
    store_results(fin, 0, pgrad_out, bgrad_out)
    store(pgrad_out.at[0], pgrad_hbm.at[0])
    store(bgrad_out, bgrad_hbm)
    store_taps(fin, dgrad_out)
    store(dgrad_out, dgrad_hbm)
    finish(stores)


def fused_step(features, depth_w, point_w, point_bias, cotangent):
    images = lax.axis_size("dp") * features.shape[0]
    cells, channels, outputs = 432, features.shape[3], point_w.shape[2]
    chunk = (CHUNK, LANES)
    scratch = [
        pltpu.VMEM((cells, channels), BF16),
        pltpu.VMEM((3, 3, 2, channels), BF16),
        pltpu.VMEM((2, channels, outputs), BF16),
        pltpu.VMEM((2, outputs), F32),
        pltpu.VMEM((cells, channels), BF16),
        pltpu.VMEM((3, 3, 2, channels), BF16),
        pltpu.VMEM((2, channels, outputs), BF16),
        pltpu.VMEM((2, outputs), F32),
        pltpu.VMEM((cells, 2 * outputs), BF16),
        pltpu.VMEM((144, channels), BF16),
        pltpu.VMEM((144, outputs), BF16),
        pltpu.VMEM((cells, outputs), BF16),
        pltpu.VMEM((cells, channels), BF16),
        pltpu.VMEM((cells, outputs), BF16),
        pltpu.VMEM((cells, outputs), BF16),
        pltpu.VMEM((cells, channels), BF16),
        pltpu.VMEM((cells, channels), BF16),
        pltpu.VMEM((channels, outputs), F32),
        pltpu.VMEM((2, 16, 8, LANES), F32),
        pltpu.VMEM((2, 2, 2, 2, 4) + chunk, BF16),
        pltpu.VMEM((2, 2, 2, 4) + chunk, BF16),
        pltpu.VMEM((2, 2, 2, 2, 4) + chunk, BF16),
        pltpu.VMEM((2, 2, 2, 4) + chunk, BF16),
        pltpu.VMEM((2, 4) + chunk, BF16),
        pltpu.VMEM((3, 2) + chunk, BF16),
        pltpu.VMEM(chunk, BF16),
        pltpu.VMEM((2, 2) + chunk, BF16),
        pltpu.VMEM((2, 2) + chunk, BF16),
        pltpu.VMEM((2,) + chunk, BF16),
        pltpu.VMEM((2,) + chunk, BF16),
        pltpu.VMEM((3,) + chunk, BF16),
        pltpu.SemaphoreType.DMA((5,)),
        pltpu.SemaphoreType.DMA((5,)),
        pltpu.SemaphoreType.DMA((SENDS,)),
        pltpu.SemaphoreType.DMA((SENDS,)),
    ]
    in_hbm = pl.BlockSpec(memory_space=pltpu.HBM)
    feature_grad, depth_grad, point_grad, bias_grad = pl.pallas_call(
        functools.partial(whole_kernel, images),
        out_shape=(
            jax.ShapeDtypeStruct((cells, channels), BF16),
            jax.ShapeDtypeStruct((3, 3, 2, channels), BF16),
            jax.ShapeDtypeStruct(point_w.shape, BF16),
            jax.ShapeDtypeStruct(point_bias.shape, F32),
        ),
        in_specs=[in_hbm] * 5,
        out_specs=[in_hbm] * 4,
        scratch_shapes=scratch,
        compiler_params=pltpu.CompilerParams(
            collective_id=0, has_side_effects=True, vmem_limit_bytes=56 * 1024 * 1024
        ),
        cost_estimate=pl.CostEstimate(flops=2 * 7 * cells * channels * outputs, bytes_accessed=8000000, transcendentals=0),
    )(features.reshape(cells, channels), jnp.transpose(depth_w, (1, 2, 0, 3)), point_w, point_bias, cotangent.reshape(cells, 2 * outputs))
    return feature_grad.reshape(features.shape), jnp.transpose(depth_grad, (2, 0, 1, 3)), point_grad, bias_grad


def fits_fused(mesh):
    return dict(mesh.shape) == {"dp": 16, "lon": 2}


def chosen_step(mesh):
    def step(features, depth_w, point_w, point_bias, cotangent):
        arguments = (features, depth_w, point_w, point_bias, cotangent)
        if fits_fused(mesh) and features.shape == (1, 9, 48, 1152) and point_w.shape[2] == 256:
            return fused_step(*arguments)
        return per_device(*arguments)

    return step


def solution(mesh):
    placed = (P("dp", "lon", None, None), P(), P(), P(), P("dp", "lon", None, None))
    return jax.shard_map(
        chosen_step(mesh),
        mesh=mesh,
        in_specs=placed,
        out_specs=(P("dp", "lon", None, None), P(), P(), P()),
        check_vma=False,
    )
```

```python
import functools

import jax
import jax.numpy as jnp
from jax import lax
from jax.experimental import pallas as pl
from jax.experimental.pallas import tpu as pltpu
from jax.sharding import PartitionSpec as P

MESH = pl.DeviceIdType.MESH
F32 = jnp.float32
BF16 = jnp.bfloat16

RATE_A = 24
RATE_B = 36


def from_behind(block, axis, distance):
    devices = range(lax.axis_size(axis))
    route = [((i - distance) % len(devices), i) for i in devices]
    return lax.ppermute(block, axis, route)


def lat_shift(grid_field, offset, axis_pos):
    height = grid_field.shape[axis_pos]
    if offset == 0:
        return grid_field
    widths = [(0, 0)] * grid_field.ndim
    if offset > 0:
        kept_rows = lax.slice_in_dim(grid_field, offset, height, axis=axis_pos)
        widths[axis_pos] = (0, offset)
    else:
        kept_rows = lax.slice_in_dim(grid_field, 0, height + offset, axis=axis_pos)
        widths[axis_pos] = (-offset, 0)
    return jnp.pad(kept_rows, widths)


def gate_slope(pre_act):
    sigmoid_val = jax.nn.sigmoid(pre_act)
    return sigmoid_val * (1.0 + pre_act * (1.0 - sigmoid_val))


def column_plan(dilation, direction, columns, group_size):
    run_list = []
    for column in range(columns):
        target = column + direction * dilation
        offset = target // columns
        local_col = target % columns
        if run_list and run_list[-1][0] == offset:
            run_list[-1][2] = local_col + 1
        else:
            run_list.append([offset, local_col, local_col + 1])
    return [(-entry[0] % group_size, entry[1], entry[2]) for entry in run_list]


def join_pieces(piece_list):
    if len(piece_list) == 1:
        return piece_list[0]
    return jnp.concatenate(piece_list, axis=1)


def fetch_each(grid_field, offset_pairs, group_size, send_fn):
    result = {}
    for offset_pair in offset_pairs:
        piece_list = []
        for shift_by, first_col, finish in column_plan(
            offset_pair[0], offset_pair[1], grid_field.shape[1], group_size
        ):
            column_piece = grid_field[:, first_col:finish]
            if shift_by != 0:
                column_piece = send_fn(column_piece, shift_by)
            piece_list.append(column_piece)
        result[offset_pair] = join_pieces(piece_list)
    return result


def send_features(column_piece, shift_by):
    return from_behind(column_piece, "lon", shift_by)


def send_grads(column_piece, shift_by):
    return from_behind(column_piece, "lon", shift_by)


def per_device(features, depth_w, point_w, point_bias, cotangent):
    group_size = lax.axis_size("lon")
    channels = features.shape[3]
    outputs = point_w.shape[2]
    dilations = (RATE_A, RATE_B)
    offset_pairs = [(dilation, direction) for dilation in dilations for direction in (-1, 1)]
    moved_in = fetch_each(features, offset_pairs, group_size, send_features)
    depth_outs = []
    for branch, dilation in enumerate(dilations):
        depth_acc = jnp.zeros(features.shape, jnp.float32)
        for lon_step in (-1, 0, 1):
            source = features if lon_step == 0 else moved_in[dilation, lon_step]
            for lat_step in (-1, 0, 1):
                tapped = lat_shift(source, lat_step * dilation, 2).astype(jnp.float32)
                depth_acc = (
                    depth_acc
                    + depth_w[branch, lat_step + 1, lon_step + 1].astype(jnp.float32) * tapped
                )
        depth_outs.append(depth_acc.astype(jnp.bfloat16))
    point_terms = []
    bias_terms = []
    dgrad_list = []
    for branch, dilation in enumerate(dilations):
        flat_depth = depth_outs[branch].reshape(-1, channels)
        point_act = (
            jnp.dot(flat_depth, point_w[branch], preferred_element_type=jnp.float32)
            + point_bias[branch]
        )
        upstream_part = (
            cotangent[..., branch * outputs : (branch + 1) * outputs]
            .reshape(-1, outputs)
            .astype(jnp.float32)
        )
        pgrad = (upstream_part * gate_slope(point_act)).astype(jnp.bfloat16)
        bias_terms.append(jnp.sum(pgrad.astype(jnp.float32), axis=0))
        point_terms.append(
            lax.dot_general(
                flat_depth, pgrad, (((0,), (0,)), ((), ())), preferred_element_type=jnp.float32
            )
        )
        dgrad = lax.dot_general(
            pgrad, point_w[branch], (((1,), (1,)), ((), ())), preferred_element_type=jnp.float32
        )
        dgrad_list.append(dgrad.astype(jnp.bfloat16).reshape(features.shape))
    point_local = jnp.stack(point_terms)
    bias_local = jnp.stack(bias_terms)
    grad_field = jnp.zeros(features.shape, jnp.float32)
    depth_terms = []
    for branch, dilation in enumerate(dilations):
        branch_pairs = [(dilation, -1), (dilation, 1)]
        moved_back = fetch_each(dgrad_list[branch], branch_pairs, group_size, send_grads)
        dgrad_wide = dgrad_list[branch].astype(jnp.float32)
        tap_rows = []
        for lat_step in (-1, 0, 1):
            tap_cols = []
            for lon_step in (-1, 0, 1):
                source = features if lon_step == 0 else moved_in[dilation, lon_step]
                tapped = lat_shift(source, lat_step * dilation, 2).astype(jnp.float32)
                tap_cols.append(jnp.sum(tapped * dgrad_wide, axis=(0, 1, 2)))
                behind = dgrad_list[branch] if lon_step == 0 else moved_back[dilation, -lon_step]
                behind = lat_shift(behind, -lat_step * dilation, 2).astype(jnp.float32)
                grad_field = (
                    grad_field
                    + depth_w[branch, lat_step + 1, lon_step + 1].astype(jnp.float32) * behind
                )
            tap_rows.append(jnp.stack(tap_cols))
        depth_terms.append(jnp.stack(tap_rows))
    depth_local = jnp.stack(depth_terms)
    feature_grad = grad_field.astype(jnp.bfloat16)
    point_sum, depth_sum, bias_sum = lax.psum((point_local, depth_local, bias_local), ("dp", "lon"))
    images = lax.axis_size("dp") * features.shape[0]
    depth_grad = (depth_sum / images).astype(jnp.bfloat16)
    point_grad = (point_sum / images).astype(jnp.bfloat16)
    bias_grad = bias_sum / images
    return (feature_grad, depth_grad, point_grad, bias_grad)


LANES = 128
CHUNK = 80
POINT_ROWS = 72
BULK = 64
SENDS = 37


def ring(e, g):
    return (g + e) % 3


def widen(block):
    wide = block.astype(F32)
    return wide[0:24], wide[24:48]


def join_rows(low, high):
    return jnp.concatenate([low, high], axis=0)


def fold(block):
    total = block[0:8]
    for at in range(8, block.shape[0], 8):
        total = total + block[at : at + 8]
    return total


def edge_taps(wide):
    rows = lax.broadcasted_iota(jnp.int32, (16, LANES), 0)
    ahead = jnp.where(rows < 12, pltpu.roll(wide[32:48], 12, 0), 0.0)
    behind = jnp.where(rows >= 4, pltpu.roll(wide[0:16], 4, 0), 0.0)
    return ahead, behind


def tap_row(dw_ref, branch, a, e, lanes):
    return dw_ref[a, e, :, lanes].astype(F32)[branch : branch + 1]


def taps_a(dw_ref, lanes):
    return [[tap_row(dw_ref, 0, a, e, lanes) for e in range(3)] for a in range(3)]


def taps_b(dw_ref, lanes):
    rows = [[tap_row(dw_ref, 1, a, e, lanes) for e in range(3)] for a in range(3)]
    return [row[0] + row[1] + row[2] for row in rows]


def lane_block(at):
    return pl.ds(pl.multiple_of(at * LANES, LANES), LANES)


def point_step(depth, weight, bias, upstream):
    act = jnp.dot(depth, weight, preferred_element_type=F32) + bias
    return (upstream.astype(F32) * gate_slope(act)).astype(BF16)


def spread_back(pgrad_ref, pw_ref, branch, out_ref):
    @pl.loop(0, 3)
    def _(at):
        cols = pl.ds(pl.multiple_of(at * 384, 384), 384)
        out_ref[:, cols] = lax.dot_general(
            pgrad_ref[...], pw_ref[branch, cols, :], (((1,), (1,)), ((), ())), preferred_element_type=F32
        ).astype(BF16)


def place(at):
    return at // 8, lax.rem(at // 4, 2), lax.rem(at, 4)


def point_terms(depth_ref, pgrad_ref, wide_ref, acc, branch):
    @pl.loop(0, 3)
    def _(at):
        cols = pl.ds(pl.multiple_of(at * 384, 384), 384)
        wide_ref[cols, :] = lax.dot_general(
            depth_ref[:, cols], pgrad_ref[...], (((0,), (0,)), ((), ())), preferred_element_type=F32
        )

    @pl.loop(0, 16)
    def _(at):
        y, x, z = place(at)
        rows = pl.ds(pl.multiple_of(at * POINT_ROWS, 8), BULK)
        for side in range(2):
            block = wide_ref[rows, side * LANES : (side + 1) * LANES]
            acc[branch, side, y, x, z, 0:BULK, :] = block.astype(BF16)


def small_terms(wide_ref, taps_ref, pgrad_ref, acc, branch):
    total = jnp.sum(pgrad_ref[...].astype(F32), axis=0, keepdims=True)
    for at in range(2):
        taps_ref[1, 9 + at, 0:1, :] = total[:, at * LANES : (at + 1) * LANES]

    @pl.loop(0, 16)
    def _(at):
        y, x, z = place(at)
        rows = pl.ds(pl.multiple_of(at * POINT_ROWS + BULK, 8), POINT_ROWS - BULK)
        for side in range(2):
            block = wide_ref[rows, side * LANES : (side + 1) * LANES]
            block = jnp.concatenate([block, taps_ref[side, at]], axis=0)
            acc[branch, side, y, x, z, BULK:CHUNK, :] = block.astype(BF16)


def store_results(fin, branch, pgrad_out, bgrad_out):
    @pl.loop(0, 8)
    def _(pair):
        y, x, z = place(pair * 2)
        rows = pl.ds(pl.multiple_of(pair * 2 * POINT_ROWS, 16), 2 * POINT_ROWS)
        for side in range(2):
            blocks = [fin[branch, side, y, x, z + k].astype(F32)[0:POINT_ROWS] for k in range(2)]
            pgrad_out[branch, rows, side * LANES : (side + 1) * LANES] = jnp.concatenate(blocks, axis=0).astype(BF16)

    for at in range(2):
        block = fin[branch, 1, 1, 0, 1 + at, BULK:CHUNK, :].astype(F32)
        bgrad_out[branch : branch + 1, at * LANES : (at + 1) * LANES] = block[8:9]


def store_taps(fin, dgrad_out):
    for at in range(9):
        lanes = slice(at * LANES, (at + 1) * LANES)
        y, x, z = at // 8, (at // 4) % 2, at % 4
        blocks = [
            [fin[branch, side, y, x, z, BULK:CHUNK, :].astype(F32)[8:16] for side in range(2)] for branch in range(2)
        ]
        for tap in range(9):
            side, row = tap // 8, tap % 8
            pair = [blocks[branch][side][row : row + 1] for branch in range(2)]
            dgrad_out[tap // 3, tap % 3, :, lanes] = jnp.concatenate(pair, axis=0).astype(BF16)


def whole_kernel(
    images, feat_hbm, dw_hbm, pw_hbm, bias_hbm, cot_hbm,
    fgrad_hbm, dgrad_hbm, pgrad_hbm, bgrad_hbm,
    fgrad_ref, dgrad_out, pgrad_out, bgrad_out,
    feat_ref, dw_ref, pw_ref, bias_ref, cot_ref,
    feat_in, cot_in, pg_in, depth_s, pg_a, pg_b, dg_a, dg_b, wide_s, taps_s,
    acc, cur, fin, r0, in_1y, in_1x, in_2x, in_2y, in_3, load_sem, store_sem, send_sem, recv_sem,
):
    dp = lax.axis_index("dp")
    my = lax.axis_index("lon")
    core = lax.rem(dp, 2)
    mx = lax.rem(dp // 2, 2)
    mz = dp // 4
    other_y = {"dp": dp, "lon": 1 - my}
    other_core = {"dp": dp + 1 - 2 * core, "lon": my}
    other_x = {"dp": dp + 2 - 4 * mx, "lon": my}
    other_z = [{"dp": lax.rem(dp + 4 * step, 16), "lon": my} for step in (1, 2, 3)]

    loads = [
        pltpu.make_async_copy(src, dst, load_sem.at[at])
        for at, (src, dst) in enumerate(
            [(feat_hbm, feat_ref), (dw_hbm, dw_ref), (pw_hbm, pw_ref), (bias_hbm, bias_ref), (cot_hbm, cot_ref)]
        )
    ]
    for copy in loads:
        copy.start()

    barrier = pltpu.get_barrier_semaphore()
    for peer in [other_y, other_core, other_x] + other_z:
        pl.semaphore_signal(barrier, inc=1, device_id=peer, device_id_type=MESH)
    pl.semaphore_wait(barrier, 6)

    numbers = iter(range(SENDS))

    def send(src, dst, peer):
        at = next(numbers)
        copy = pltpu.make_async_remote_copy(
            src_ref=src, dst_ref=dst, send_sem=send_sem.at[at], recv_sem=recv_sem.at[at],
            device_id=peer, device_id_type=MESH,
        )
        copy.start()
        return copy

    stores = []

    def store(src, dst):
        copy = pltpu.make_async_copy(src, dst, store_sem.at[len(stores)])
        copy.start()
        stores.append(copy)

    def finish(copies):
        for copy in copies:
            copy.wait()

    feat_copy = send(feat_hbm.at[144:288], feat_in, other_y)
    cot_copy = send(cot_hbm.at[144:288, 0:256], cot_in, other_y)
    finish(loads)
    taps_s[...] = jnp.zeros_like(taps_s)

    def add_into(at, extra):
        cur[at] = (cur[at].astype(F32) + extra.astype(F32)).astype(BF16)

    def share(index, peer):
        return send(fin.at[index], fin.at[index], peer)

    def send_half(branch, rows):
        return send(acc.at[branch, 1 - core, :, :, :, rows], r0.at[branch, :, :, :, rows], other_core)

    def add_halves(branch):
        @pl.loop(0, 4)
        def _(z):
            for y in range(2):
                for x in range(2):
                    total = acc[branch, core, y, x, z].astype(F32) + r0[branch, y, x, z].astype(F32)
                    cur[branch, y, x, z] = total.astype(BF16)

    every = slice(None)
    lower, upper = pl.ds(0, 2), pl.ds(2, 2)

    def reduce_1(branch):
        add_halves(branch)
        return [
            send(cur.at[branch, 1 - my, :, lower], in_1y.at[branch], other_y),
            send(cur.at[branch, :, 1 - mx, upper], in_1x.at[branch], other_x),
        ]

    def reduce_2(branch):
        for k in range(2):
            for z in range(2):
                add_into((branch, my, k, z), in_1y[branch, k, z])
                add_into((branch, k, mx, 2 + z), in_1x[branch, k, z])
        return [
            send(cur.at[branch, my, 1 - mx, lower], in_2x.at[branch], other_x),
            send(cur.at[branch, 1 - my, mx, upper], in_2y.at[branch], other_y),
        ]

    def reduce_3(branch):
        for z in range(2):
            add_into((branch, my, mx, z), in_2x[branch, z])
            add_into((branch, my, mx, 2 + z), in_2y[branch, z])
        return [
            send(cur.at[branch, my, mx, lax.rem(mz + k + 1, 4)], in_3.at[branch, k], other_z[k]) for k in range(3)
        ]

    def gather_1(branch):
        total = cur[branch, my, mx, mz].astype(F32)
        for k in range(3):
            total = total + in_3[branch, k].astype(F32)
        fin[branch, core, my, mx, mz] = (total * (1.0 / images)).astype(BF16)
        return [share((branch, core, my, mx, mz), peer) for peer in other_z]

    def gather_2(branch):
        return [
            share((branch, core, my, mx, lower), other_x),
            share((branch, core, my, mx, upper), other_y),
        ]

    def gather_3(branch):
        return [
            share((branch, core, my, every, lower), other_y),
            share((branch, core, every, mx, upper), other_x),
        ]

    def gather_4(branch):
        return [share((branch, core), other_core)]

    @pl.loop(0, 9)
    def _(at):
        lanes = lane_block(at)
        w = taps_b(dw_ref, lanes)
        for col in range(9):
            rows = pl.ds(col * 48, 48)
            wide = feat_ref[rows, lanes].astype(F32)
            ahead, behind = edge_taps(wide)
            low = w[1] * wide[0:16] + w[2] * ahead
            high = w[1] * wide[32:48] + w[0] * behind
            depth = jnp.concatenate([low, w[1] * wide[16:32], high], axis=0)
            depth_s[rows, lanes] = depth.astype(BF16)

    pg_b[...] = point_step(depth_s[...], pw_ref[1], bias_ref[1:2, :], cot_ref[:, 256:512])
    point_terms(depth_s, pg_b, wide_s, acc, 1)
    b_step = [send_half(1, pl.ds(0, BULK))]
    spread_back(pg_b, pw_ref, 1, dg_b)

    @pl.loop(0, 9)
    def _(at):
        lanes = lane_block(at)
        sums = [jnp.zeros((8, LANES), F32) for _ in range(3)]
        for col in range(9):
            rows = pl.ds(col * 48, 48)
            wide = feat_ref[rows, lanes].astype(F32)
            grad = dg_b[rows, lanes].astype(F32)
            ahead, behind = edge_taps(wide)
            sums[0] = sums[0] + fold(behind * grad[32:48])
            sums[1] = sums[1] + fold(wide * grad)
            sums[2] = sums[2] + fold(ahead * grad[0:16])
        for a in range(3):
            total = jnp.sum(sums[a], axis=0, keepdims=True)
            for e in range(3):
                tap = 3 * a + e
                taps_s[tap // 8, at, tap % 8 : tap % 8 + 1, :] = total

    small_terms(wide_s, taps_s, pg_b, acc, 1)
    b_step.append(send_half(1, pl.ds(BULK, CHUNK - BULK)))
    finish(b_step)
    b_step = reduce_1(1)

    feat_copy.wait()

    def cell_rows(g, t):
        return pl.ds((3 * g + t) * 48, 48)

    def load_feat(g, t, lanes):
        if g == 2:
            return widen(feat_in[pl.ds(t * 48, 48), lanes])
        return widen(feat_ref[pl.ds((6 * g + t) * 48, 48), lanes])

    @pl.loop(0, 9)
    def _(at):
        lanes = lane_block(at)
        w = taps_a(dw_ref, lanes)
        for t in range(3):
            cells = [load_feat(g, t, lanes) for g in range(3)]
            for g in range(3):
                low = high = 0.0
                for e in (-1, 0, 1):
                    src_low, src_high = cells[ring(e, g)]
                    low = low + w[1][e + 1] * src_low + w[2][e + 1] * src_high
                    high = high + w[1][e + 1] * src_high + w[0][e + 1] * src_low
                depth_s[cell_rows(g, t), lanes] = join_rows(low, high).astype(BF16)

    finish(b_step)
    b_step = reduce_2(1)

    cot_copy.wait()
    for g in range(3):
        rows = pl.ds(144 * g, 144)
        upstream = cot_in[...] if g == 2 else cot_ref[pl.ds(288 * g, 144), 0:256]
        pg_a[rows, :] = point_step(depth_s[rows, :], pw_ref[0], bias_ref[0:1, :], upstream)
    pg_copy = send(pg_a, pg_in, other_y)

    finish(b_step)
    b_step = reduce_3(1)

    point_terms(depth_s, pg_a, wide_s, acc, 0)
    a_step = [send_half(0, pl.ds(0, BULK))]

    finish(b_step)
    b_step = gather_1(1)

    spread_back(pg_a, pw_ref, 0, dg_a)

    @pl.loop(0, 9)
    def _(at):
        lanes = lane_block(at)
        sums = [[jnp.zeros((8, LANES), F32) for _ in range(3)] for _ in range(3)]
        for t in range(3):
            cells = [load_feat(g, t, lanes) for g in range(3)]
            for g in range(3):
                grad_low, grad_high = widen(dg_a[cell_rows(g, t), lanes])
                for e in (-1, 0, 1):
                    src_low, src_high = cells[ring(e, g)]
                    sums[0][e + 1] = sums[0][e + 1] + fold(src_low * grad_high)
                    sums[1][e + 1] = sums[1][e + 1] + fold(src_low * grad_low + src_high * grad_high)
                    sums[2][e + 1] = sums[2][e + 1] + fold(src_high * grad_low)
        for a in range(3):
            for e in range(3):
                tap = 3 * a + e
                taps_s[tap // 8, at, tap % 8 : tap % 8 + 1, :] = jnp.sum(sums[a][e], axis=0, keepdims=True)

    small_terms(wide_s, taps_s, pg_a, acc, 0)
    a_step.append(send_half(0, pl.ds(BULK, CHUNK - BULK)))

    finish(b_step)
    b_step = gather_2(1)

    finish(a_step)
    a_step = reduce_1(0)

    def branch_b_grad(rows, lanes, w):
        grad = dg_b[rows, lanes].astype(F32)
        ahead, behind = edge_taps(grad)
        low = w[1] * grad[0:16] + w[0] * ahead
        high = w[1] * grad[32:48] + w[2] * behind
        return jnp.concatenate([low, w[1] * grad[16:32], high], axis=0)

    def branch_a_grad(w, grads, g):
        low = high = 0.0
        for e in (-1, 0, 1):
            src_low, src_high = grads[ring(-e, g)]
            low = low + w[1][e + 1] * src_low + w[0][e + 1] * src_high
            high = high + w[1][e + 1] * src_high + w[2][e + 1] * src_low
        return join_rows(low, high)

    @pl.loop(0, 9)
    def _(at):
        lanes = lane_block(at)
        w = taps_a(dw_ref, lanes)
        wb = taps_b(dw_ref, lanes)
        for t in range(3):
            grads = [widen(dg_a[cell_rows(g, t), lanes]) for g in range(3)]
            for g in range(2):
                rows = pl.ds((6 * g + t) * 48, 48)
                total = branch_a_grad(w, grads, g) + branch_b_grad(rows, lanes, wb)
                fgrad_ref[rows, lanes] = total.astype(BF16)

    finish(b_step)
    b_step = gather_3(1)

    finish(a_step)
    a_step = reduce_2(0)

    pg_copy.wait()
    spread_back(pg_in, pw_ref, 0, dg_a)

    @pl.loop(0, 9)
    def _(at):
        lanes = lane_block(at)
        w = taps_a(dw_ref, lanes)
        wb = taps_b(dw_ref, lanes)
        for t in range(3):
            grads = [widen(dg_a[cell_rows(g, t), lanes]) for g in range(3)]
            rows = pl.ds((3 + t) * 48, 48)
            total = branch_a_grad(w, grads, 2) + branch_b_grad(rows, lanes, wb)
            fgrad_ref[rows, lanes] = total.astype(BF16)

    store(fgrad_ref, fgrad_hbm)

    finish(a_step)
    a_step = reduce_3(0)

    finish(b_step)
    b_step = gather_4(1)

    finish(a_step)
    a_step = gather_1(0)

    finish(b_step)
    store_results(fin, 1, pgrad_out, bgrad_out)
    store(pgrad_out.at[1], pgrad_hbm.at[1])

    finish(a_step)
    a_step = gather_2(0)
    finish(a_step)
    a_step = gather_3(0)
    finish(a_step)
    finish(gather_4(0))
    store_results(fin, 0, pgrad_out, bgrad_out)
    store(pgrad_out.at[0], pgrad_hbm.at[0])
    store(bgrad_out, bgrad_hbm)
    store_taps(fin, dgrad_out)
    store(dgrad_out, dgrad_hbm)
    finish(stores)


def fused_step(features, depth_w, point_w, point_bias, cotangent):
    images = lax.axis_size("dp") * features.shape[0]
    cells, channels, outputs = 432, features.shape[3], point_w.shape[2]
    chunk = (CHUNK, LANES)
    scratch = [
        pltpu.VMEM((cells, channels), BF16),
        pltpu.VMEM((3, 3, 2, channels), BF16),
        pltpu.VMEM((2, channels, outputs), BF16),
        pltpu.VMEM((2, outputs), F32),
        pltpu.VMEM((cells, channels), BF16),
        pltpu.VMEM((3, 3, 2, channels), BF16),
        pltpu.VMEM((2, channels, outputs), BF16),
        pltpu.VMEM((2, outputs), F32),
        pltpu.VMEM((cells, 2 * outputs), BF16),
        pltpu.VMEM((144, channels), BF16),
        pltpu.VMEM((144, outputs), BF16),
        pltpu.VMEM((cells, outputs), BF16),
        pltpu.VMEM((cells, channels), BF16),
        pltpu.VMEM((cells, outputs), BF16),
        pltpu.VMEM((cells, outputs), BF16),
        pltpu.VMEM((cells, channels), BF16),
        pltpu.VMEM((cells, channels), BF16),
        pltpu.VMEM((channels, outputs), F32),
        pltpu.VMEM((2, 16, 8, LANES), F32),
        pltpu.VMEM((2, 2, 2, 2, 4) + chunk, BF16),
        pltpu.VMEM((2, 2, 2, 4) + chunk, BF16),
        pltpu.VMEM((2, 2, 2, 2, 4) + chunk, BF16),
        pltpu.VMEM((2, 2, 2, 4) + chunk, BF16),
        pltpu.VMEM((2, 2, 2) + chunk, BF16),
        pltpu.VMEM((2, 2, 2) + chunk, BF16),
        pltpu.VMEM((2, 2) + chunk, BF16),
        pltpu.VMEM((2, 2) + chunk, BF16),
        pltpu.VMEM((2, 3) + chunk, BF16),
        pltpu.SemaphoreType.DMA((5,)),
        pltpu.SemaphoreType.DMA((5,)),
        pltpu.SemaphoreType.DMA((SENDS,)),
        pltpu.SemaphoreType.DMA((SENDS,)),
    ]
    in_hbm = pl.BlockSpec(memory_space=pltpu.HBM)
    feature_grad, depth_grad, point_grad, bias_grad = pl.pallas_call(
        functools.partial(whole_kernel, images),
        out_shape=(
            jax.ShapeDtypeStruct((cells, channels), BF16),
            jax.ShapeDtypeStruct((3, 3, 2, channels), BF16),
            jax.ShapeDtypeStruct(point_w.shape, BF16),
            jax.ShapeDtypeStruct(point_bias.shape, F32),
        ),
        in_specs=[in_hbm] * 5,
        out_specs=[in_hbm] * 4,
        scratch_shapes=scratch,
        compiler_params=pltpu.CompilerParams(
            collective_id=0, has_side_effects=True, vmem_limit_bytes=56 * 1024 * 1024
        ),
        cost_estimate=pl.CostEstimate(flops=2 * 7 * cells * channels * outputs, bytes_accessed=8000000, transcendentals=0),
    )(features.reshape(cells, channels), jnp.transpose(depth_w, (1, 2, 0, 3)), point_w, point_bias, cotangent.reshape(cells, 2 * outputs))
    return feature_grad.reshape(features.shape), jnp.transpose(depth_grad, (2, 0, 1, 3)), point_grad, bias_grad


def fits_fused(mesh):
    return dict(mesh.shape) == {"dp": 16, "lon": 2}


def chosen_step(mesh):
    def step(features, depth_w, point_w, point_bias, cotangent):
        arguments = (features, depth_w, point_w, point_bias, cotangent)
        if fits_fused(mesh) and features.shape == (1, 9, 48, 1152) and point_w.shape[2] == 256:
            return fused_step(*arguments)
        return per_device(*arguments)

    return step


def solution(mesh):
    placed = (P("dp", "lon", None, None), P(), P(), P(), P("dp", "lon", None, None))
    return jax.shard_map(
        chosen_step(mesh),
        mesh=mesh,
        in_specs=placed,
        out_specs=(P("dp", "lon", None, None), P(), P(), P()),
        check_vma=False,
    )
```

```python
import functools

import jax
import jax.numpy as jnp
from jax import lax
from jax.experimental import pallas as pl
from jax.experimental.pallas import tpu as pltpu
from jax.sharding import PartitionSpec as P

MESH = pl.DeviceIdType.MESH
F32 = jnp.float32
BF16 = jnp.bfloat16

RATE_A = 24
RATE_B = 36


def from_behind(block, axis, distance):
    devices = range(lax.axis_size(axis))
    route = [((i - distance) % len(devices), i) for i in devices]
    return lax.ppermute(block, axis, route)


def lat_shift(grid_field, offset, axis_pos):
    height = grid_field.shape[axis_pos]
    if offset == 0:
        return grid_field
    widths = [(0, 0)] * grid_field.ndim
    if offset > 0:
        kept_rows = lax.slice_in_dim(grid_field, offset, height, axis=axis_pos)
        widths[axis_pos] = (0, offset)
    else:
        kept_rows = lax.slice_in_dim(grid_field, 0, height + offset, axis=axis_pos)
        widths[axis_pos] = (-offset, 0)
    return jnp.pad(kept_rows, widths)


def gate_slope(pre_act):
    sigmoid_val = jax.nn.sigmoid(pre_act)
    return sigmoid_val * (1.0 + pre_act * (1.0 - sigmoid_val))


def column_plan(dilation, direction, columns, group_size):
    run_list = []
    for column in range(columns):
        target = column + direction * dilation
        offset = target // columns
        local_col = target % columns
        if run_list and run_list[-1][0] == offset:
            run_list[-1][2] = local_col + 1
        else:
            run_list.append([offset, local_col, local_col + 1])
    return [(-entry[0] % group_size, entry[1], entry[2]) for entry in run_list]


def join_pieces(piece_list):
    if len(piece_list) == 1:
        return piece_list[0]
    return jnp.concatenate(piece_list, axis=1)


def fetch_each(grid_field, offset_pairs, group_size, send_fn):
    result = {}
    for offset_pair in offset_pairs:
        piece_list = []
        for shift_by, first_col, finish in column_plan(
            offset_pair[0], offset_pair[1], grid_field.shape[1], group_size
        ):
            column_piece = grid_field[:, first_col:finish]
            if shift_by != 0:
                column_piece = send_fn(column_piece, shift_by)
            piece_list.append(column_piece)
        result[offset_pair] = join_pieces(piece_list)
    return result


def send_features(column_piece, shift_by):
    return from_behind(column_piece, "lon", shift_by)


def send_grads(column_piece, shift_by):
    return from_behind(column_piece, "lon", shift_by)


def per_device(features, depth_w, point_w, point_bias, cotangent):
    group_size = lax.axis_size("lon")
    channels = features.shape[3]
    outputs = point_w.shape[2]
    dilations = (RATE_A, RATE_B)
    offset_pairs = [(dilation, direction) for dilation in dilations for direction in (-1, 1)]
    moved_in = fetch_each(features, offset_pairs, group_size, send_features)
    depth_outs = []
    for branch, dilation in enumerate(dilations):
        depth_acc = jnp.zeros(features.shape, jnp.float32)
        for lon_step in (-1, 0, 1):
            source = features if lon_step == 0 else moved_in[dilation, lon_step]
            for lat_step in (-1, 0, 1):
                tapped = lat_shift(source, lat_step * dilation, 2).astype(jnp.float32)
                depth_acc = (
                    depth_acc
                    + depth_w[branch, lat_step + 1, lon_step + 1].astype(jnp.float32) * tapped
                )
        depth_outs.append(depth_acc.astype(jnp.bfloat16))
    point_terms = []
    bias_terms = []
    dgrad_list = []
    for branch, dilation in enumerate(dilations):
        flat_depth = depth_outs[branch].reshape(-1, channels)
        point_act = (
            jnp.dot(flat_depth, point_w[branch], preferred_element_type=jnp.float32)
            + point_bias[branch]
        )
        upstream_part = (
            cotangent[..., branch * outputs : (branch + 1) * outputs]
            .reshape(-1, outputs)
            .astype(jnp.float32)
        )
        pgrad = (upstream_part * gate_slope(point_act)).astype(jnp.bfloat16)
        bias_terms.append(jnp.sum(pgrad.astype(jnp.float32), axis=0))
        point_terms.append(
            lax.dot_general(
                flat_depth, pgrad, (((0,), (0,)), ((), ())), preferred_element_type=jnp.float32
            )
        )
        dgrad = lax.dot_general(
            pgrad, point_w[branch], (((1,), (1,)), ((), ())), preferred_element_type=jnp.float32
        )
        dgrad_list.append(dgrad.astype(jnp.bfloat16).reshape(features.shape))
    point_local = jnp.stack(point_terms)
    bias_local = jnp.stack(bias_terms)
    grad_field = jnp.zeros(features.shape, jnp.float32)
    depth_terms = []
    for branch, dilation in enumerate(dilations):
        branch_pairs = [(dilation, -1), (dilation, 1)]
        moved_back = fetch_each(dgrad_list[branch], branch_pairs, group_size, send_grads)
        dgrad_wide = dgrad_list[branch].astype(jnp.float32)
        tap_rows = []
        for lat_step in (-1, 0, 1):
            tap_cols = []
            for lon_step in (-1, 0, 1):
                source = features if lon_step == 0 else moved_in[dilation, lon_step]
                tapped = lat_shift(source, lat_step * dilation, 2).astype(jnp.float32)
                tap_cols.append(jnp.sum(tapped * dgrad_wide, axis=(0, 1, 2)))
                behind = dgrad_list[branch] if lon_step == 0 else moved_back[dilation, -lon_step]
                behind = lat_shift(behind, -lat_step * dilation, 2).astype(jnp.float32)
                grad_field = (
                    grad_field
                    + depth_w[branch, lat_step + 1, lon_step + 1].astype(jnp.float32) * behind
                )
            tap_rows.append(jnp.stack(tap_cols))
        depth_terms.append(jnp.stack(tap_rows))
    depth_local = jnp.stack(depth_terms)
    feature_grad = grad_field.astype(jnp.bfloat16)
    point_sum, depth_sum, bias_sum = lax.psum((point_local, depth_local, bias_local), ("dp", "lon"))
    images = lax.axis_size("dp") * features.shape[0]
    depth_grad = (depth_sum / images).astype(jnp.bfloat16)
    point_grad = (point_sum / images).astype(jnp.bfloat16)
    bias_grad = bias_sum / images
    return (feature_grad, depth_grad, point_grad, bias_grad)


LANES = 128
CHUNK = 80
POINT_ROWS = 72
BULK = 64
SENDS = 42


def ring(e, g):
    return (g + e) % 3


def widen(block):
    wide = block.astype(F32)
    return wide[0:24], wide[24:48]


def join_rows(low, high):
    return jnp.concatenate([low, high], axis=0)


def fold(block):
    total = block[0:8]
    for at in range(8, block.shape[0], 8):
        total = total + block[at : at + 8]
    return total


def edge_taps(wide):
    rows = lax.broadcasted_iota(jnp.int32, (16, LANES), 0)
    ahead = jnp.where(rows < 12, pltpu.roll(wide[32:48], 12, 0), 0.0)
    behind = jnp.where(rows >= 4, pltpu.roll(wide[0:16], 4, 0), 0.0)
    return ahead, behind


def tap_row(dw_ref, branch, a, e, lanes):
    return dw_ref[a, e, :, lanes].astype(F32)[branch : branch + 1]


def taps_a(dw_ref, lanes):
    return [[tap_row(dw_ref, 0, a, e, lanes) for e in range(3)] for a in range(3)]


def taps_b(dw_ref, lanes):
    rows = [[tap_row(dw_ref, 1, a, e, lanes) for e in range(3)] for a in range(3)]
    return [row[0] + row[1] + row[2] for row in rows]


def lane_block(at):
    return pl.ds(pl.multiple_of(at * LANES, LANES), LANES)


def point_step(depth, weight, bias, upstream):
    act = jnp.dot(depth, weight, preferred_element_type=F32) + bias
    return (upstream.astype(F32) * gate_slope(act)).astype(BF16)


def spread_back(pgrad_ref, pw_ref, branch, out_ref):
    @pl.loop(0, 3)
    def _(at):
        cols = pl.ds(pl.multiple_of(at * 384, 384), 384)
        out_ref[:, cols] = lax.dot_general(
            pgrad_ref[...], pw_ref[branch, cols, :], (((1,), (1,)), ((), ())), preferred_element_type=F32
        ).astype(BF16)


def place(at):
    return at // 8, lax.rem(at // 4, 2), lax.rem(at, 4)


def point_terms(depth_ref, pgrad_ref, wide_ref, acc, branch):
    @pl.loop(0, 3)
    def _(at):
        cols = pl.ds(pl.multiple_of(at * 384, 384), 384)
        wide_ref[cols, :] = lax.dot_general(
            depth_ref[:, cols], pgrad_ref[...], (((0,), (0,)), ((), ())), preferred_element_type=F32
        )

    @pl.loop(0, 16)
    def _(at):
        y, x, z = place(at)
        rows = pl.ds(pl.multiple_of(at * POINT_ROWS, 8), BULK)
        for side in range(2):
            block = wide_ref[rows, side * LANES : (side + 1) * LANES]
            acc[branch, side, y, x, z, 0:BULK, :] = block.astype(BF16)


def small_terms(wide_ref, taps_ref, pgrad_ref, acc, branch):
    total = jnp.sum(pgrad_ref[...].astype(F32), axis=0, keepdims=True)
    for at in range(2):
        taps_ref[1, 9 + at, 0:1, :] = total[:, at * LANES : (at + 1) * LANES]

    @pl.loop(0, 16)
    def _(at):
        y, x, z = place(at)
        rows = pl.ds(pl.multiple_of(at * POINT_ROWS + BULK, 8), POINT_ROWS - BULK)
        for side in range(2):
            block = wide_ref[rows, side * LANES : (side + 1) * LANES]
            block = jnp.concatenate([block, taps_ref[side, at]], axis=0)
            acc[branch, side, y, x, z, BULK:CHUNK, :] = block.astype(BF16)


def store_results(fin, branch, pgrad_out, bgrad_out):
    @pl.loop(0, 8)
    def _(pair):
        y, x, z = place(pair * 2)
        rows = pl.ds(pl.multiple_of(pair * 2 * POINT_ROWS, 16), 2 * POINT_ROWS)
        for side in range(2):
            blocks = [fin[branch, side, y, x, z + k].astype(F32)[0:POINT_ROWS] for k in range(2)]
            pgrad_out[branch, rows, side * LANES : (side + 1) * LANES] = jnp.concatenate(blocks, axis=0).astype(BF16)

    for at in range(2):
        block = fin[branch, 1, 1, 0, 1 + at, BULK:CHUNK, :].astype(F32)
        bgrad_out[branch : branch + 1, at * LANES : (at + 1) * LANES] = block[8:9]


def store_taps(fin, dgrad_out):
    for at in range(9):
        lanes = slice(at * LANES, (at + 1) * LANES)
        y, x, z = at // 8, (at // 4) % 2, at % 4
        blocks = [
            [fin[branch, side, y, x, z, BULK:CHUNK, :].astype(F32)[8:16] for side in range(2)] for branch in range(2)
        ]
        for tap in range(9):
            side, row = tap // 8, tap % 8
            pair = [blocks[branch][side][row : row + 1] for branch in range(2)]
            dgrad_out[tap // 3, tap % 3, :, lanes] = jnp.concatenate(pair, axis=0).astype(BF16)


def whole_kernel(
    images, feat_hbm, dw_hbm, pw_hbm, bias_hbm, cot_hbm,
    fgrad_hbm, dgrad_hbm, pgrad_hbm, bgrad_hbm,
    fgrad_ref, dgrad_out, pgrad_out, bgrad_out,
    feat_ref, dw_ref, pw_ref, bias_ref, cot_ref,
    feat_in, cot_in, pg_in, depth_s, pg_a, pg_b, dg_a, dg_b, wide_s, taps_s,
    acc, cur, fin, r0, in_all, in_plane, in_z, load_sem, store_sem, send_sem, recv_sem,
):
    dp = lax.axis_index("dp")
    my = lax.axis_index("lon")
    core = lax.rem(dp, 2)
    mx = lax.rem(dp // 2, 2)
    mz = dp // 4
    other_y = {"dp": dp, "lon": 1 - my}
    other_core = {"dp": dp + 1 - 2 * core, "lon": my}
    other_z = [{"dp": lax.rem(dp + 4 * step, 16), "lon": my} for step in (1, 2, 3)]

    me = my * 8 + mx * 4 + mz

    def owner(at):
        y, x, z = place(at)
        return {"dp": (z * 2 + x) * 2 + core, "lon": y}

    owners = [lax.rem(me + step, 16) for step in range(1, 16)]
    plane = [(1 - my, mx), (my, 1 - mx), (1 - my, 1 - mx)]
    plane_peers = [{"dp": (mz * 2 + x) * 2 + core, "lon": y} for y, x in plane]

    loads = [
        pltpu.make_async_copy(src, dst, load_sem.at[at])
        for at, (src, dst) in enumerate(
            [(feat_hbm, feat_ref), (dw_hbm, dw_ref), (pw_hbm, pw_ref), (bias_hbm, bias_ref), (cot_hbm, cot_ref)]
        )
    ]
    for copy in loads:
        copy.start()

    barrier = pltpu.get_barrier_semaphore()
    for peer in [owner(at) for at in owners] + [other_core]:
        pl.semaphore_signal(barrier, inc=1, device_id=peer, device_id_type=MESH)
    pl.semaphore_wait(barrier, 16)

    numbers = iter(range(SENDS))

    def send(src, dst, peer):
        at = next(numbers)
        copy = pltpu.make_async_remote_copy(
            src_ref=src, dst_ref=dst, send_sem=send_sem.at[at], recv_sem=recv_sem.at[at],
            device_id=peer, device_id_type=MESH,
        )
        copy.start()
        return copy

    stores = []

    def store(src, dst):
        copy = pltpu.make_async_copy(src, dst, store_sem.at[len(stores)])
        copy.start()
        stores.append(copy)

    def finish(copies):
        for copy in copies:
            copy.wait()

    feat_copy = send(feat_hbm.at[144:288], feat_in, other_y)
    cot_copy = send(cot_hbm.at[144:288, 0:256], cot_in, other_y)
    finish(loads)
    taps_s[...] = jnp.zeros_like(taps_s)

    def share(index, peer):
        return send(fin.at[index], fin.at[index], peer)

    def send_half(branch, rows):
        return send(acc.at[branch, 1 - core, :, :, :, rows], r0.at[branch, :, :, :, rows], other_core)

    def add_halves(branch):
        @pl.loop(0, 4)
        def _(z):
            for y in range(2):
                for x in range(2):
                    total = acc[branch, core, y, x, z].astype(F32) + r0[branch, y, x, z].astype(F32)
                    cur[branch, y, x, z] = total.astype(BF16)

    def scatter_all(branch):
        add_halves(branch)
        return [send(cur.at[(branch,) + place(at)], in_all.at[k], owner(at)) for k, at in enumerate(owners)]

    def scatter_plane(branch):
        add_halves(branch)
        return [
            send(cur.at[branch, y, x], in_plane.at[k], peer) for k, ((y, x), peer) in enumerate(zip(plane, plane_peers))
        ]

    def scatter_z(branch):
        @pl.loop(0, 4)
        def _(z):
            total = cur[branch, my, mx, z].astype(F32)
            for k in range(3):
                total = total + in_plane[k, z].astype(F32)
            cur[branch, my, mx, z] = total.astype(BF16)

        return [
            send(cur.at[branch, my, mx, lax.rem(mz + k + 1, 4)], in_z.at[k], other_z[k]) for k in range(3)
        ]

    def settle(branch, arrived):
        total = cur[branch, my, mx, mz].astype(F32)
        for k in range(arrived.shape[0]):
            total = total + arrived[k].astype(F32)
        fin[branch, core, my, mx, mz] = (total * (1.0 / images)).astype(BF16)

    def gather_z(branch):
        return [share((branch, core, my, mx, mz), peer) for peer in other_z]

    def gather_plane(branch):
        return [share((branch, core, my, mx), peer) for peer in plane_peers]

    def gather_core(branch):
        return [share((branch, core), other_core)]

    @pl.loop(0, 9)
    def _(at):
        lanes = lane_block(at)
        w = taps_b(dw_ref, lanes)
        for col in range(9):
            rows = pl.ds(col * 48, 48)
            wide = feat_ref[rows, lanes].astype(F32)
            ahead, behind = edge_taps(wide)
            low = w[1] * wide[0:16] + w[2] * ahead
            high = w[1] * wide[32:48] + w[0] * behind
            depth = jnp.concatenate([low, w[1] * wide[16:32], high], axis=0)
            depth_s[rows, lanes] = depth.astype(BF16)

    pg_b[...] = point_step(depth_s[...], pw_ref[1], bias_ref[1:2, :], cot_ref[:, 256:512])
    point_terms(depth_s, pg_b, wide_s, acc, 1)
    b_step = [send_half(1, pl.ds(0, BULK))]
    spread_back(pg_b, pw_ref, 1, dg_b)

    @pl.loop(0, 9)
    def _(at):
        lanes = lane_block(at)
        sums = [jnp.zeros((8, LANES), F32) for _ in range(3)]
        for col in range(9):
            rows = pl.ds(col * 48, 48)
            wide = feat_ref[rows, lanes].astype(F32)
            grad = dg_b[rows, lanes].astype(F32)
            ahead, behind = edge_taps(wide)
            sums[0] = sums[0] + fold(behind * grad[32:48])
            sums[1] = sums[1] + fold(wide * grad)
            sums[2] = sums[2] + fold(ahead * grad[0:16])
        for a in range(3):
            total = jnp.sum(sums[a], axis=0, keepdims=True)
            for e in range(3):
                tap = 3 * a + e
                taps_s[tap // 8, at, tap % 8 : tap % 8 + 1, :] = total

    small_terms(wide_s, taps_s, pg_b, acc, 1)
    b_step.append(send_half(1, pl.ds(BULK, CHUNK - BULK)))

    feat_copy.wait()
    finish(b_step)
    b_step = scatter_all(1)

    def cell_rows(g, t):
        return pl.ds((3 * g + t) * 48, 48)

    def load_feat(g, t, lanes):
        if g == 2:
            return widen(feat_in[pl.ds(t * 48, 48), lanes])
        return widen(feat_ref[pl.ds((6 * g + t) * 48, 48), lanes])

    @pl.loop(0, 9)
    def _(at):
        lanes = lane_block(at)
        w = taps_a(dw_ref, lanes)
        for t in range(3):
            cells = [load_feat(g, t, lanes) for g in range(3)]
            for g in range(3):
                low = high = 0.0
                for e in (-1, 0, 1):
                    src_low, src_high = cells[ring(e, g)]
                    low = low + w[1][e + 1] * src_low + w[2][e + 1] * src_high
                    high = high + w[1][e + 1] * src_high + w[0][e + 1] * src_low
                depth_s[cell_rows(g, t), lanes] = join_rows(low, high).astype(BF16)

    cot_copy.wait()
    for g in range(3):
        rows = pl.ds(144 * g, 144)
        upstream = cot_in[...] if g == 2 else cot_ref[pl.ds(288 * g, 144), 0:256]
        pg_a[rows, :] = point_step(depth_s[rows, :], pw_ref[0], bias_ref[0:1, :], upstream)
    pg_copy = send(pg_a, pg_in, other_y)

    point_terms(depth_s, pg_a, wide_s, acc, 0)
    a_step = [send_half(0, pl.ds(0, BULK))]
    spread_back(pg_a, pw_ref, 0, dg_a)

    @pl.loop(0, 9)
    def _(at):
        lanes = lane_block(at)
        sums = [[jnp.zeros((8, LANES), F32) for _ in range(3)] for _ in range(3)]
        for t in range(3):
            cells = [load_feat(g, t, lanes) for g in range(3)]
            for g in range(3):
                grad_low, grad_high = widen(dg_a[cell_rows(g, t), lanes])
                for e in (-1, 0, 1):
                    src_low, src_high = cells[ring(e, g)]
                    sums[0][e + 1] = sums[0][e + 1] + fold(src_low * grad_high)
                    sums[1][e + 1] = sums[1][e + 1] + fold(src_low * grad_low + src_high * grad_high)
                    sums[2][e + 1] = sums[2][e + 1] + fold(src_high * grad_low)
        for a in range(3):
            for e in range(3):
                tap = 3 * a + e
                taps_s[tap // 8, at, tap % 8 : tap % 8 + 1, :] = jnp.sum(sums[a][e], axis=0, keepdims=True)

    small_terms(wide_s, taps_s, pg_a, acc, 0)
    a_step.append(send_half(0, pl.ds(BULK, CHUNK - BULK)))

    finish(b_step)
    settle(1, in_all)
    b_step = gather_z(1)

    finish(a_step)
    a_step = scatter_plane(0)

    def branch_b_grad(rows, lanes, w):
        grad = dg_b[rows, lanes].astype(F32)
        ahead, behind = edge_taps(grad)
        low = w[1] * grad[0:16] + w[0] * ahead
        high = w[1] * grad[32:48] + w[2] * behind
        return jnp.concatenate([low, w[1] * grad[16:32], high], axis=0)

    def branch_a_grad(w, grads, g):
        low = high = 0.0
        for e in (-1, 0, 1):
            src_low, src_high = grads[ring(-e, g)]
            low = low + w[1][e + 1] * src_low + w[0][e + 1] * src_high
            high = high + w[1][e + 1] * src_high + w[2][e + 1] * src_low
        return join_rows(low, high)

    @pl.loop(0, 9)
    def _(at):
        lanes = lane_block(at)
        w = taps_a(dw_ref, lanes)
        wb = taps_b(dw_ref, lanes)
        for t in range(3):
            grads = [widen(dg_a[cell_rows(g, t), lanes]) for g in range(3)]
            for g in range(2):
                rows = pl.ds((6 * g + t) * 48, 48)
                total = branch_a_grad(w, grads, g) + branch_b_grad(rows, lanes, wb)
                fgrad_ref[rows, lanes] = total.astype(BF16)

    finish(a_step)
    a_step = scatter_z(0)

    finish(b_step)
    b_step = gather_plane(1)

    pg_copy.wait()
    spread_back(pg_in, pw_ref, 0, dg_a)

    @pl.loop(0, 9)
    def _(at):
        lanes = lane_block(at)
        w = taps_a(dw_ref, lanes)
        wb = taps_b(dw_ref, lanes)
        for t in range(3):
            grads = [widen(dg_a[cell_rows(g, t), lanes]) for g in range(3)]
            rows = pl.ds((3 + t) * 48, 48)
            total = branch_a_grad(w, grads, 2) + branch_b_grad(rows, lanes, wb)
            fgrad_ref[rows, lanes] = total.astype(BF16)

    store(fgrad_ref, fgrad_hbm)

    finish(a_step)
    settle(0, in_z)
    a_step = gather_z(0)

    finish(b_step)
    b_step = gather_core(1)

    finish(a_step)
    a_step = gather_plane(0)

    finish(b_step)
    store_results(fin, 1, pgrad_out, bgrad_out)
    store(pgrad_out.at[1], pgrad_hbm.at[1])

    finish(a_step)
    finish(gather_core(0))
    store_results(fin, 0, pgrad_out, bgrad_out)
    store(pgrad_out.at[0], pgrad_hbm.at[0])
    store(bgrad_out, bgrad_hbm)
    store_taps(fin, dgrad_out)
    store(dgrad_out, dgrad_hbm)
    finish(stores)


def fused_step(features, depth_w, point_w, point_bias, cotangent):
    images = lax.axis_size("dp") * features.shape[0]
    cells, channels, outputs = 432, features.shape[3], point_w.shape[2]
    chunk = (CHUNK, LANES)
    scratch = [
        pltpu.VMEM((cells, channels), BF16),
        pltpu.VMEM((3, 3, 2, channels), BF16),
        pltpu.VMEM((2, channels, outputs), BF16),
        pltpu.VMEM((2, outputs), F32),
        pltpu.VMEM((cells, channels), BF16),
        pltpu.VMEM((3, 3, 2, channels), BF16),
        pltpu.VMEM((2, channels, outputs), BF16),
        pltpu.VMEM((2, outputs), F32),
        pltpu.VMEM((cells, 2 * outputs), BF16),
        pltpu.VMEM((144, channels), BF16),
        pltpu.VMEM((144, outputs), BF16),
        pltpu.VMEM((cells, outputs), BF16),
        pltpu.VMEM((cells, channels), BF16),
        pltpu.VMEM((cells, outputs), BF16),
        pltpu.VMEM((cells, outputs), BF16),
        pltpu.VMEM((cells, channels), BF16),
        pltpu.VMEM((cells, channels), BF16),
        pltpu.VMEM((channels, outputs), F32),
        pltpu.VMEM((2, 16, 8, LANES), F32),
        pltpu.VMEM((2, 2, 2, 2, 4) + chunk, BF16),
        pltpu.VMEM((2, 2, 2, 4) + chunk, BF16),
        pltpu.VMEM((2, 2, 2, 2, 4) + chunk, BF16),
        pltpu.VMEM((2, 2, 2, 4) + chunk, BF16),
        pltpu.VMEM((15,) + chunk, BF16),
        pltpu.VMEM((3, 4) + chunk, BF16),
        pltpu.VMEM((3,) + chunk, BF16),
        pltpu.SemaphoreType.DMA((5,)),
        pltpu.SemaphoreType.DMA((5,)),
        pltpu.SemaphoreType.DMA((SENDS,)),
        pltpu.SemaphoreType.DMA((SENDS,)),
    ]
    in_hbm = pl.BlockSpec(memory_space=pltpu.HBM)
    feature_grad, depth_grad, point_grad, bias_grad = pl.pallas_call(
        functools.partial(whole_kernel, images),
        out_shape=(
            jax.ShapeDtypeStruct((cells, channels), BF16),
            jax.ShapeDtypeStruct((3, 3, 2, channels), BF16),
            jax.ShapeDtypeStruct(point_w.shape, BF16),
            jax.ShapeDtypeStruct(point_bias.shape, F32),
        ),
        in_specs=[in_hbm] * 5,
        out_specs=[in_hbm] * 4,
        scratch_shapes=scratch,
        compiler_params=pltpu.CompilerParams(
            collective_id=0, has_side_effects=True, vmem_limit_bytes=56 * 1024 * 1024
        ),
        cost_estimate=pl.CostEstimate(flops=2 * 7 * cells * channels * outputs, bytes_accessed=8000000, transcendentals=0),
    )(features.reshape(cells, channels), jnp.transpose(depth_w, (1, 2, 0, 3)), point_w, point_bias, cotangent.reshape(cells, 2 * outputs))
    return feature_grad.reshape(features.shape), jnp.transpose(depth_grad, (2, 0, 1, 3)), point_grad, bias_grad


def fits_fused(mesh):
    return dict(mesh.shape) == {"dp": 16, "lon": 2}


def chosen_step(mesh):
    def step(features, depth_w, point_w, point_bias, cotangent):
        arguments = (features, depth_w, point_w, point_bias, cotangent)
        if fits_fused(mesh) and features.shape == (1, 9, 48, 1152) and point_w.shape[2] == 256:
            return fused_step(*arguments)
        return per_device(*arguments)

    return step


def solution(mesh):
    placed = (P("dp", "lon", None, None), P(), P(), P(), P("dp", "lon", None, None))
    return jax.shard_map(
        chosen_step(mesh),
        mesh=mesh,
        in_specs=placed,
        out_specs=(P("dp", "lon", None, None), P(), P(), P()),
        check_vma=False,
    )
```

```python
import functools

import jax
import jax.numpy as jnp
from jax import lax
from jax.experimental import pallas as pl
from jax.experimental.pallas import tpu as pltpu
from jax.sharding import PartitionSpec as P

MESH = pl.DeviceIdType.MESH
F32 = jnp.float32
BF16 = jnp.bfloat16

RATE_A = 24
RATE_B = 36


def from_behind(block, axis, distance):
    devices = range(lax.axis_size(axis))
    route = [((i - distance) % len(devices), i) for i in devices]
    return lax.ppermute(block, axis, route)


def lat_shift(grid_field, offset, axis_pos):
    height = grid_field.shape[axis_pos]
    if offset == 0:
        return grid_field
    widths = [(0, 0)] * grid_field.ndim
    if offset > 0:
        kept_rows = lax.slice_in_dim(grid_field, offset, height, axis=axis_pos)
        widths[axis_pos] = (0, offset)
    else:
        kept_rows = lax.slice_in_dim(grid_field, 0, height + offset, axis=axis_pos)
        widths[axis_pos] = (-offset, 0)
    return jnp.pad(kept_rows, widths)


def gate_slope(pre_act):
    sigmoid_val = jax.nn.sigmoid(pre_act)
    return sigmoid_val * (1.0 + pre_act * (1.0 - sigmoid_val))


def column_plan(dilation, direction, columns, group_size):
    run_list = []
    for column in range(columns):
        target = column + direction * dilation
        offset = target // columns
        local_col = target % columns
        if run_list and run_list[-1][0] == offset:
            run_list[-1][2] = local_col + 1
        else:
            run_list.append([offset, local_col, local_col + 1])
    return [(-entry[0] % group_size, entry[1], entry[2]) for entry in run_list]


def join_pieces(piece_list):
    if len(piece_list) == 1:
        return piece_list[0]
    return jnp.concatenate(piece_list, axis=1)


def fetch_each(grid_field, offset_pairs, group_size, send_fn):
    result = {}
    for offset_pair in offset_pairs:
        piece_list = []
        for shift_by, first_col, finish in column_plan(
            offset_pair[0], offset_pair[1], grid_field.shape[1], group_size
        ):
            column_piece = grid_field[:, first_col:finish]
            if shift_by != 0:
                column_piece = send_fn(column_piece, shift_by)
            piece_list.append(column_piece)
        result[offset_pair] = join_pieces(piece_list)
    return result


def send_features(column_piece, shift_by):
    return from_behind(column_piece, "lon", shift_by)


def send_grads(column_piece, shift_by):
    return from_behind(column_piece, "lon", shift_by)


def per_device(features, depth_w, point_w, point_bias, cotangent):
    group_size = lax.axis_size("lon")
    channels = features.shape[3]
    outputs = point_w.shape[2]
    dilations = (RATE_A, RATE_B)
    offset_pairs = [(dilation, direction) for dilation in dilations for direction in (-1, 1)]
    moved_in = fetch_each(features, offset_pairs, group_size, send_features)
    depth_outs = []
    for branch, dilation in enumerate(dilations):
        depth_acc = jnp.zeros(features.shape, jnp.float32)
        for lon_step in (-1, 0, 1):
            source = features if lon_step == 0 else moved_in[dilation, lon_step]
            for lat_step in (-1, 0, 1):
                tapped = lat_shift(source, lat_step * dilation, 2).astype(jnp.float32)
                depth_acc = (
                    depth_acc
                    + depth_w[branch, lat_step + 1, lon_step + 1].astype(jnp.float32) * tapped
                )
        depth_outs.append(depth_acc.astype(jnp.bfloat16))
    point_terms = []
    bias_terms = []
    dgrad_list = []
    for branch, dilation in enumerate(dilations):
        flat_depth = depth_outs[branch].reshape(-1, channels)
        point_act = (
            jnp.dot(flat_depth, point_w[branch], preferred_element_type=jnp.float32)
            + point_bias[branch]
        )
        upstream_part = (
            cotangent[..., branch * outputs : (branch + 1) * outputs]
            .reshape(-1, outputs)
            .astype(jnp.float32)
        )
        pgrad = (upstream_part * gate_slope(point_act)).astype(jnp.bfloat16)
        bias_terms.append(jnp.sum(pgrad.astype(jnp.float32), axis=0))
        point_terms.append(
            lax.dot_general(
                flat_depth, pgrad, (((0,), (0,)), ((), ())), preferred_element_type=jnp.float32
            )
        )
        dgrad = lax.dot_general(
            pgrad, point_w[branch], (((1,), (1,)), ((), ())), preferred_element_type=jnp.float32
        )
        dgrad_list.append(dgrad.astype(jnp.bfloat16).reshape(features.shape))
    point_local = jnp.stack(point_terms)
    bias_local = jnp.stack(bias_terms)
    grad_field = jnp.zeros(features.shape, jnp.float32)
    depth_terms = []
    for branch, dilation in enumerate(dilations):
        branch_pairs = [(dilation, -1), (dilation, 1)]
        moved_back = fetch_each(dgrad_list[branch], branch_pairs, group_size, send_grads)
        dgrad_wide = dgrad_list[branch].astype(jnp.float32)
        tap_rows = []
        for lat_step in (-1, 0, 1):
            tap_cols = []
            for lon_step in (-1, 0, 1):
                source = features if lon_step == 0 else moved_in[dilation, lon_step]
                tapped = lat_shift(source, lat_step * dilation, 2).astype(jnp.float32)
                tap_cols.append(jnp.sum(tapped * dgrad_wide, axis=(0, 1, 2)))
                behind = dgrad_list[branch] if lon_step == 0 else moved_back[dilation, -lon_step]
                behind = lat_shift(behind, -lat_step * dilation, 2).astype(jnp.float32)
                grad_field = (
                    grad_field
                    + depth_w[branch, lat_step + 1, lon_step + 1].astype(jnp.float32) * behind
                )
            tap_rows.append(jnp.stack(tap_cols))
        depth_terms.append(jnp.stack(tap_rows))
    depth_local = jnp.stack(depth_terms)
    feature_grad = grad_field.astype(jnp.bfloat16)
    point_sum, depth_sum, bias_sum = lax.psum((point_local, depth_local, bias_local), ("dp", "lon"))
    images = lax.axis_size("dp") * features.shape[0]
    depth_grad = (depth_sum / images).astype(jnp.bfloat16)
    point_grad = (point_sum / images).astype(jnp.bfloat16)
    bias_grad = bias_sum / images
    return (feature_grad, depth_grad, point_grad, bias_grad)


LANES = 128
CHUNK = 80
POINT_ROWS = 72
BULK = 64
SENDS = 55


def ring(e, g):
    return (g + e) % 3


def widen(block):
    wide = block.astype(F32)
    return wide[0:24], wide[24:48]


def join_rows(low, high):
    return jnp.concatenate([low, high], axis=0)


def fold(block):
    total = block[0:8]
    for at in range(8, block.shape[0], 8):
        total = total + block[at : at + 8]
    return total


def edge_taps(wide):
    rows = lax.broadcasted_iota(jnp.int32, (16, LANES), 0)
    ahead = jnp.where(rows < 12, pltpu.roll(wide[32:48], 12, 0), 0.0)
    behind = jnp.where(rows >= 4, pltpu.roll(wide[0:16], 4, 0), 0.0)
    return ahead, behind


def tap_row(dw_ref, branch, a, e, lanes):
    return dw_ref[a, e, :, lanes].astype(F32)[branch : branch + 1]


def taps_a(dw_ref, lanes):
    return [[tap_row(dw_ref, 0, a, e, lanes) for e in range(3)] for a in range(3)]


def taps_b(dw_ref, lanes):
    rows = [[tap_row(dw_ref, 1, a, e, lanes) for e in range(3)] for a in range(3)]
    return [row[0] + row[1] + row[2] for row in rows]


def lane_block(at):
    return pl.ds(pl.multiple_of(at * LANES, LANES), LANES)


def point_step(depth, weight, bias, upstream):
    act = jnp.dot(depth, weight, preferred_element_type=F32) + bias
    return (upstream.astype(F32) * gate_slope(act)).astype(BF16)


def spread_back(pgrad_ref, pw_ref, branch, out_ref):
    @pl.loop(0, 3)
    def _(at):
        cols = pl.ds(pl.multiple_of(at * 384, 384), 384)
        out_ref[:, cols] = lax.dot_general(
            pgrad_ref[...], pw_ref[branch, cols, :], (((1,), (1,)), ((), ())), preferred_element_type=F32
        ).astype(BF16)


def place(at):
    return at // 8, lax.rem(at // 4, 2), lax.rem(at, 4)


def point_terms(depth_ref, pgrad_ref, wide_ref, acc, branch):
    @pl.loop(0, 3)
    def _(at):
        cols = pl.ds(pl.multiple_of(at * 384, 384), 384)
        wide_ref[cols, :] = lax.dot_general(
            depth_ref[:, cols], pgrad_ref[...], (((0,), (0,)), ((), ())), preferred_element_type=F32
        )

    @pl.loop(0, 16)
    def _(at):
        y, x, z = place(at)
        rows = pl.ds(pl.multiple_of(at * POINT_ROWS, 8), BULK)
        for side in range(2):
            block = wide_ref[rows, side * LANES : (side + 1) * LANES]
            acc[branch, side, y, x, z, 0:BULK, :] = block.astype(BF16)


def small_terms(wide_ref, taps_ref, pgrad_ref, acc, branch):
    total = jnp.sum(pgrad_ref[...].astype(F32), axis=0, keepdims=True)
    for at in range(2):
        taps_ref[1, 9 + at, 0:1, :] = total[:, at * LANES : (at + 1) * LANES]

    @pl.loop(0, 16)
    def _(at):
        y, x, z = place(at)
        rows = pl.ds(pl.multiple_of(at * POINT_ROWS + BULK, 8), POINT_ROWS - BULK)
        for side in range(2):
            block = wide_ref[rows, side * LANES : (side + 1) * LANES]
            block = jnp.concatenate([block, taps_ref[side, at]], axis=0)
            acc[branch, side, y, x, z, BULK:CHUNK, :] = block.astype(BF16)


def store_results(fin, branch, pgrad_out, bgrad_out):
    @pl.loop(0, 8)
    def _(pair):
        y, x, z = place(pair * 2)
        rows = pl.ds(pl.multiple_of(pair * 2 * POINT_ROWS, 16), 2 * POINT_ROWS)
        for side in range(2):
            blocks = [fin[branch, side, y, x, z + k].astype(F32)[0:POINT_ROWS] for k in range(2)]
            pgrad_out[branch, rows, side * LANES : (side + 1) * LANES] = jnp.concatenate(blocks, axis=0).astype(BF16)

    for at in range(2):
        block = fin[branch, 1, 1, 0, 1 + at, BULK:CHUNK, :].astype(F32)
        bgrad_out[branch : branch + 1, at * LANES : (at + 1) * LANES] = block[8:9]


def store_taps(fin, dgrad_out):
    for at in range(9):
        lanes = slice(at * LANES, (at + 1) * LANES)
        y, x, z = at // 8, (at // 4) % 2, at % 4
        blocks = [
            [fin[branch, side, y, x, z, BULK:CHUNK, :].astype(F32)[8:16] for side in range(2)] for branch in range(2)
        ]
        for tap in range(9):
            side, row = tap // 8, tap % 8
            pair = [blocks[branch][side][row : row + 1] for branch in range(2)]
            dgrad_out[tap // 3, tap % 3, :, lanes] = jnp.concatenate(pair, axis=0).astype(BF16)


def whole_kernel(
    images, feat_hbm, dw_hbm, pw_hbm, bias_hbm, cot_hbm,
    fgrad_hbm, dgrad_hbm, pgrad_hbm, bgrad_hbm,
    fgrad_ref, dgrad_out, pgrad_out, bgrad_out,
    feat_ref, dw_ref, pw_ref, bias_ref, cot_ref,
    feat_in, cot_in, pg_in, depth_s, pg_a, pg_b, dg_a, dg_b, wide_s, taps_s,
    acc, cur, fin, r0, in_all, in_plane, in_z, load_sem, store_sem, send_sem, recv_sem,
):
    dp = lax.axis_index("dp")
    my = lax.axis_index("lon")
    core = lax.rem(dp, 2)
    mx = lax.rem(dp // 2, 2)
    mz = dp // 4
    other_y = {"dp": dp, "lon": 1 - my}
    other_core = {"dp": dp + 1 - 2 * core, "lon": my}
    other_z = [{"dp": lax.rem(dp + 4 * step, 16), "lon": my} for step in (1, 2, 3)]

    me = my * 8 + mx * 4 + mz

    def owner(at):
        y, x, z = place(at)
        return {"dp": (z * 2 + x) * 2 + core, "lon": y}

    owners = [lax.rem(me + step, 16) for step in range(1, 16)]
    plane = [(1 - my, mx), (my, 1 - mx), (1 - my, 1 - mx)]
    plane_peers = [{"dp": (mz * 2 + x) * 2 + core, "lon": y} for y, x in plane]

    loads = [
        pltpu.make_async_copy(src, dst, load_sem.at[at])
        for at, (src, dst) in enumerate(
            [(feat_hbm, feat_ref), (dw_hbm, dw_ref), (pw_hbm, pw_ref), (bias_hbm, bias_ref), (cot_hbm, cot_ref)]
        )
    ]
    for copy in loads:
        copy.start()

    barrier = pltpu.get_barrier_semaphore()
    for peer in [owner(at) for at in owners] + [other_core]:
        pl.semaphore_signal(barrier, inc=1, device_id=peer, device_id_type=MESH)
    pl.semaphore_wait(barrier, 16)

    numbers = iter(range(SENDS))

    def send(src, dst, peer):
        at = next(numbers)
        copy = pltpu.make_async_remote_copy(
            src_ref=src, dst_ref=dst, send_sem=send_sem.at[at], recv_sem=recv_sem.at[at],
            device_id=peer, device_id_type=MESH,
        )
        copy.start()
        return copy

    stores = []

    def store(src, dst):
        copy = pltpu.make_async_copy(src, dst, store_sem.at[len(stores)])
        copy.start()
        stores.append(copy)

    def finish(copies):
        for copy in copies:
            copy.wait()

    feat_copy = send(feat_hbm.at[144:288], feat_in, other_y)
    cot_copy = send(cot_hbm.at[144:288, 0:256], cot_in, other_y)
    finish(loads)
    taps_s[...] = jnp.zeros_like(taps_s)

    def share(index, peer):
        return send(fin.at[index], fin.at[index], peer)

    def send_half(branch, rows):
        return send(acc.at[branch, 1 - core, :, :, :, rows], r0.at[branch, :, :, :, rows], other_core)

    whole_rows, bulk_rows, tail_rows = pl.ds(0, CHUNK), pl.ds(0, BULK), pl.ds(BULK, CHUNK - BULK)

    def add_halves(branch, rows):
        @pl.loop(0, 4)
        def _(z):
            for y in range(2):
                for x in range(2):
                    total = acc[branch, core, y, x, z, rows].astype(F32) + r0[branch, y, x, z, rows].astype(F32)
                    cur[branch, y, x, z, rows] = total.astype(BF16)

    def scatter_all(branch):
        add_halves(branch, whole_rows)
        return [send(cur.at[(branch,) + place(at)], in_all.at[k], owner(at)) for k, at in enumerate(owners)]

    def scatter_plane(branch, rows):
        add_halves(branch, rows)
        return [
            send(cur.at[branch, y, x, :, rows], in_plane.at[k, :, rows], peer)
            for k, ((y, x), peer) in enumerate(zip(plane, plane_peers))
        ]

    def scatter_z(branch, rows):
        @pl.loop(0, 4)
        def _(z):
            total = cur[branch, my, mx, z, rows].astype(F32)
            for k in range(3):
                total = total + in_plane[k, z, rows].astype(F32)
            cur[branch, my, mx, z, rows] = total.astype(BF16)

        return [
            send(cur.at[branch, my, mx, lax.rem(mz + k + 1, 4), rows], in_z.at[k, rows], other_z[k]) for k in range(3)
        ]

    def settle(branch, arrived, rows):
        total = cur[branch, my, mx, mz, rows].astype(F32)
        for k in range(arrived.shape[0]):
            total = total + arrived[k, rows].astype(F32)
        fin[branch, core, my, mx, mz, rows] = (total * (1.0 / images)).astype(BF16)

    every = slice(None)

    def gather_z(branch, rows):
        return [share((branch, core, my, mx, mz, rows), peer) for peer in other_z]

    def gather_plane(branch, rows):
        return [share((branch, core, my, mx, every, rows), peer) for peer in plane_peers]

    def gather_core(branch, rows):
        return [share((branch, core, every, every, every, rows), other_core)]

    @pl.loop(0, 9)
    def _(at):
        lanes = lane_block(at)
        w = taps_b(dw_ref, lanes)
        for col in range(9):
            rows = pl.ds(col * 48, 48)
            wide = feat_ref[rows, lanes].astype(F32)
            ahead, behind = edge_taps(wide)
            low = w[1] * wide[0:16] + w[2] * ahead
            high = w[1] * wide[32:48] + w[0] * behind
            depth = jnp.concatenate([low, w[1] * wide[16:32], high], axis=0)
            depth_s[rows, lanes] = depth.astype(BF16)

    pg_b[...] = point_step(depth_s[...], pw_ref[1], bias_ref[1:2, :], cot_ref[:, 256:512])
    point_terms(depth_s, pg_b, wide_s, acc, 1)
    b_step = [send_half(1, pl.ds(0, BULK))]
    spread_back(pg_b, pw_ref, 1, dg_b)

    @pl.loop(0, 9)
    def _(at):
        lanes = lane_block(at)
        sums = [jnp.zeros((8, LANES), F32) for _ in range(3)]
        for col in range(9):
            rows = pl.ds(col * 48, 48)
            wide = feat_ref[rows, lanes].astype(F32)
            grad = dg_b[rows, lanes].astype(F32)
            ahead, behind = edge_taps(wide)
            sums[0] = sums[0] + fold(behind * grad[32:48])
            sums[1] = sums[1] + fold(wide * grad)
            sums[2] = sums[2] + fold(ahead * grad[0:16])
        for a in range(3):
            total = jnp.sum(sums[a], axis=0, keepdims=True)
            for e in range(3):
                tap = 3 * a + e
                taps_s[tap // 8, at, tap % 8 : tap % 8 + 1, :] = total

    small_terms(wide_s, taps_s, pg_b, acc, 1)
    b_step.append(send_half(1, pl.ds(BULK, CHUNK - BULK)))

    feat_copy.wait()
    finish(b_step)
    b_step = scatter_all(1)

    def cell_rows(g, t):
        return pl.ds((3 * g + t) * 48, 48)

    def load_feat(g, t, lanes):
        if g == 2:
            return widen(feat_in[pl.ds(t * 48, 48), lanes])
        return widen(feat_ref[pl.ds((6 * g + t) * 48, 48), lanes])

    @pl.loop(0, 9)
    def _(at):
        lanes = lane_block(at)
        w = taps_a(dw_ref, lanes)
        for t in range(3):
            cells = [load_feat(g, t, lanes) for g in range(3)]
            for g in range(3):
                low = high = 0.0
                for e in (-1, 0, 1):
                    src_low, src_high = cells[ring(e, g)]
                    low = low + w[1][e + 1] * src_low + w[2][e + 1] * src_high
                    high = high + w[1][e + 1] * src_high + w[0][e + 1] * src_low
                depth_s[cell_rows(g, t), lanes] = join_rows(low, high).astype(BF16)

    cot_copy.wait()
    for g in range(3):
        rows = pl.ds(144 * g, 144)
        upstream = cot_in[...] if g == 2 else cot_ref[pl.ds(288 * g, 144), 0:256]
        pg_a[rows, :] = point_step(depth_s[rows, :], pw_ref[0], bias_ref[0:1, :], upstream)
    pg_copy = send(pg_a, pg_in, other_y)

    point_terms(depth_s, pg_a, wide_s, acc, 0)
    a_step = [send_half(0, pl.ds(0, BULK))]
    spread_back(pg_a, pw_ref, 0, dg_a)

    finish(a_step)
    a_step = scatter_plane(0, bulk_rows)

    @pl.loop(0, 9)
    def _(at):
        lanes = lane_block(at)
        sums = [[jnp.zeros((8, LANES), F32) for _ in range(3)] for _ in range(3)]
        for t in range(3):
            cells = [load_feat(g, t, lanes) for g in range(3)]
            for g in range(3):
                grad_low, grad_high = widen(dg_a[cell_rows(g, t), lanes])
                for e in (-1, 0, 1):
                    src_low, src_high = cells[ring(e, g)]
                    sums[0][e + 1] = sums[0][e + 1] + fold(src_low * grad_high)
                    sums[1][e + 1] = sums[1][e + 1] + fold(src_low * grad_low + src_high * grad_high)
                    sums[2][e + 1] = sums[2][e + 1] + fold(src_high * grad_low)
        for a in range(3):
            for e in range(3):
                tap = 3 * a + e
                taps_s[tap // 8, at, tap % 8 : tap % 8 + 1, :] = jnp.sum(sums[a][e], axis=0, keepdims=True)

    small_terms(wide_s, taps_s, pg_a, acc, 0)
    a_tail = [send_half(0, tail_rows)]

    finish(b_step)
    settle(1, in_all, whole_rows)
    b_step = gather_z(1, whole_rows)

    finish(a_step)
    a_step = scatter_z(0, bulk_rows)
    finish(a_tail)
    a_tail = scatter_plane(0, tail_rows)

    def branch_b_grad(rows, lanes, w):
        grad = dg_b[rows, lanes].astype(F32)
        ahead, behind = edge_taps(grad)
        low = w[1] * grad[0:16] + w[0] * ahead
        high = w[1] * grad[32:48] + w[2] * behind
        return jnp.concatenate([low, w[1] * grad[16:32], high], axis=0)

    def branch_a_grad(w, grads, g):
        low = high = 0.0
        for e in (-1, 0, 1):
            src_low, src_high = grads[ring(-e, g)]
            low = low + w[1][e + 1] * src_low + w[0][e + 1] * src_high
            high = high + w[1][e + 1] * src_high + w[2][e + 1] * src_low
        return join_rows(low, high)

    @pl.loop(0, 9)
    def _(at):
        lanes = lane_block(at)
        w = taps_a(dw_ref, lanes)
        wb = taps_b(dw_ref, lanes)
        for t in range(3):
            grads = [widen(dg_a[cell_rows(g, t), lanes]) for g in range(3)]
            for g in range(2):
                rows = pl.ds((6 * g + t) * 48, 48)
                total = branch_a_grad(w, grads, g) + branch_b_grad(rows, lanes, wb)
                fgrad_ref[rows, lanes] = total.astype(BF16)

    finish(a_step)
    settle(0, in_z, bulk_rows)
    a_step = gather_z(0, bulk_rows)
    finish(a_tail)
    a_tail = scatter_z(0, tail_rows)

    finish(b_step)
    b_step = gather_plane(1, whole_rows)

    pg_copy.wait()
    spread_back(pg_in, pw_ref, 0, dg_a)

    @pl.loop(0, 9)
    def _(at):
        lanes = lane_block(at)
        w = taps_a(dw_ref, lanes)
        wb = taps_b(dw_ref, lanes)
        for t in range(3):
            grads = [widen(dg_a[cell_rows(g, t), lanes]) for g in range(3)]
            rows = pl.ds((3 + t) * 48, 48)
            total = branch_a_grad(w, grads, 2) + branch_b_grad(rows, lanes, wb)
            fgrad_ref[rows, lanes] = total.astype(BF16)

    store(fgrad_ref, fgrad_hbm)

    finish(a_step)
    a_step = gather_plane(0, bulk_rows)
    finish(a_tail)
    settle(0, in_z, tail_rows)
    a_tail = gather_z(0, tail_rows)

    finish(b_step)
    b_step = gather_core(1, whole_rows)

    finish(a_tail)
    a_tail = gather_plane(0, tail_rows)
    finish(a_step)
    a_step = gather_core(0, bulk_rows)

    finish(b_step)
    store_results(fin, 1, pgrad_out, bgrad_out)
    store(pgrad_out.at[1], pgrad_hbm.at[1])

    finish(a_tail)
    a_tail = gather_core(0, tail_rows)
    finish(a_step)
    finish(a_tail)
    store_results(fin, 0, pgrad_out, bgrad_out)
    store(pgrad_out.at[0], pgrad_hbm.at[0])
    store(bgrad_out, bgrad_hbm)
    store_taps(fin, dgrad_out)
    store(dgrad_out, dgrad_hbm)
    finish(stores)


def fused_step(features, depth_w, point_w, point_bias, cotangent):
    images = lax.axis_size("dp") * features.shape[0]
    cells, channels, outputs = 432, features.shape[3], point_w.shape[2]
    chunk = (CHUNK, LANES)
    scratch = [
        pltpu.VMEM((cells, channels), BF16),
        pltpu.VMEM((3, 3, 2, channels), BF16),
        pltpu.VMEM((2, channels, outputs), BF16),
        pltpu.VMEM((2, outputs), F32),
        pltpu.VMEM((cells, channels), BF16),
        pltpu.VMEM((3, 3, 2, channels), BF16),
        pltpu.VMEM((2, channels, outputs), BF16),
        pltpu.VMEM((2, outputs), F32),
        pltpu.VMEM((cells, 2 * outputs), BF16),
        pltpu.VMEM((144, channels), BF16),
        pltpu.VMEM((144, outputs), BF16),
        pltpu.VMEM((cells, outputs), BF16),
        pltpu.VMEM((cells, channels), BF16),
        pltpu.VMEM((cells, outputs), BF16),
        pltpu.VMEM((cells, outputs), BF16),
        pltpu.VMEM((cells, channels), BF16),
        pltpu.VMEM((cells, channels), BF16),
        pltpu.VMEM((channels, outputs), F32),
        pltpu.VMEM((2, 16, 8, LANES), F32),
        pltpu.VMEM((2, 2, 2, 2, 4) + chunk, BF16),
        pltpu.VMEM((2, 2, 2, 4) + chunk, BF16),
        pltpu.VMEM((2, 2, 2, 2, 4) + chunk, BF16),
        pltpu.VMEM((2, 2, 2, 4) + chunk, BF16),
        pltpu.VMEM((15,) + chunk, BF16),
        pltpu.VMEM((3, 4) + chunk, BF16),
        pltpu.VMEM((3,) + chunk, BF16),
        pltpu.SemaphoreType.DMA((5,)),
        pltpu.SemaphoreType.DMA((5,)),
        pltpu.SemaphoreType.DMA((SENDS,)),
        pltpu.SemaphoreType.DMA((SENDS,)),
    ]
    in_hbm = pl.BlockSpec(memory_space=pltpu.HBM)
    feature_grad, depth_grad, point_grad, bias_grad = pl.pallas_call(
        functools.partial(whole_kernel, images),
        out_shape=(
            jax.ShapeDtypeStruct((cells, channels), BF16),
            jax.ShapeDtypeStruct((3, 3, 2, channels), BF16),
            jax.ShapeDtypeStruct(point_w.shape, BF16),
            jax.ShapeDtypeStruct(point_bias.shape, F32),
        ),
        in_specs=[in_hbm] * 5,
        out_specs=[in_hbm] * 4,
        scratch_shapes=scratch,
        compiler_params=pltpu.CompilerParams(
            collective_id=0, has_side_effects=True, vmem_limit_bytes=56 * 1024 * 1024
        ),
        cost_estimate=pl.CostEstimate(flops=2 * 7 * cells * channels * outputs, bytes_accessed=8000000, transcendentals=0),
    )(features.reshape(cells, channels), jnp.transpose(depth_w, (1, 2, 0, 3)), point_w, point_bias, cotangent.reshape(cells, 2 * outputs))
    return feature_grad.reshape(features.shape), jnp.transpose(depth_grad, (2, 0, 1, 3)), point_grad, bias_grad


def fits_fused(mesh):
    return dict(mesh.shape) == {"dp": 16, "lon": 2}


def chosen_step(mesh):
    def step(features, depth_w, point_w, point_bias, cotangent):
        arguments = (features, depth_w, point_w, point_bias, cotangent)
        if fits_fused(mesh) and features.shape == (1, 9, 48, 1152) and point_w.shape[2] == 256:
            return fused_step(*arguments)
        return per_device(*arguments)

    return step


def solution(mesh):
    placed = (P("dp", "lon", None, None), P(), P(), P(), P("dp", "lon", None, None))
    return jax.shard_map(
        chosen_step(mesh),
        mesh=mesh,
        in_specs=placed,
        out_specs=(P("dp", "lon", None, None), P(), P(), P()),
        check_vma=False,
    )
```
